512 devices in a mesh: tok: 2 (over core), row: 16 (over x, y), col: 16 (over z).
Axes of the slice: x: 4, y: 4, z: 16, core: 2. Of those that a mesh axis runs over, the one named last changes fastest.
Arguments:
- tokens: bfloat16 [512, 16384], P(('tok', 'col'), 'row'), may hold values from -6 to 6
- w1_blocks: bfloat16 [16, 16, 18, 128, 128], P('row', 'col'), may hold values from -0.1875 to 0.1875
- w1_coords: int32 [16, 16, 18, 2], P('row', 'col'), may hold values from 0 to 31, as said below
- w1_count: int32 [16, 16], P('row', 'col'), may hold values from 2 to 18, as said below
- w2_blocks: bfloat16 [16, 16, 18, 128, 128], P('row', 'col'), may hold values from -0.09375 to 0.09375
- w2_coords: int32 [16, 16, 18, 2], P('row', 'col'), may hold values from 0 to 31, as said below
- w2_count: int32 [16, 16], P('row', 'col'), may hold values from 2 to 18, as said below
- cotangent: bfloat16 [512, 16384], P(('tok', 'col'), 'row'), may hold values from -6 to 6
Outputs:
- output: bfloat16 [512, 16384], P(('tok', 'col'), 'row')
- input_grad: bfloat16 [512, 16384], P(('tok', 'col'), 'row')
- w1_grad: bfloat16 [16, 16, 18, 128, 128], P('row', 'col')
- w2_grad: bfloat16 [16, 16, 18, 128, 128], P('row', 'col')
The draws below stay inside these ranges and needn't reach their ends.
Inputs may be any that keep to these rules, and one draw needn't show every extreme that they name: `w1_coords`: within one tile all 18 slots name distinct blocks; the first entry lies below 8 and the second below 32. `w2_coords`: within one tile all 18 slots name distinct blocks; the first entry lies below 32 and the second below 8. `w1_count`: some tile lists 18 blocks. `w2_count`: some tile lists 18 blocks.
All inputs are finite; a program needn't handle non-finite values.
Results may differ from the reference program's by a relative error of at most 0.022.
Values may be sent and summed in bfloat16 or wider, within the bound.
No kernel may reach another device: no remote copies, remote signals or barrier semaphores. Data moves between devices by JAX's collectives and lax.ppermute only.
A program may use at most 64 MiB of HBM per device.

```python
import jax
import jax.numpy as jnp
from jax import lax

D = 16384
F = 65536
BS = 128
TOK = 256
NB = 18
TOKENS = 512
DB = 8
HB = 32
N_TOK = 2
N_ROW = 16
N_COL = 16


def draw_picks(key):
    keys = jax.random.split(key, N_ROW * N_COL)
    return jax.vmap(lambda single: jax.random.permutation(single, DB * HB)[:NB])(keys)


def draw_counts(key):
    first, second = jax.random.split(key)
    counts = jax.random.randint(first, (N_ROW * N_COL,), max(1, NB // 8), NB + 1)
    chosen = jax.random.randint(second, (), 0, N_ROW * N_COL)
    counts = jnp.where(jnp.arange(N_ROW * N_COL) == chosen, NB, counts)
    return counts.reshape(N_ROW, N_COL).astype(jnp.int32)


def draw_w1_coords(key, part):
    key = jax.random.fold_in(key, 11)
    picks = draw_picks(key)
    coords = jnp.stack([picks // HB, picks % HB], axis=-1)
    return coords.reshape(N_ROW, N_COL, NB, 2).astype(jnp.int32)


def draw_w2_coords(key, part):
    key = jax.random.fold_in(key, 12)
    picks = draw_picks(key)
    coords = jnp.stack([picks // DB, picks % DB], axis=-1)
    return coords.reshape(N_ROW, N_COL, NB, 2).astype(jnp.int32)


def draw_w1_count(key, part):
    key = jax.random.fold_in(key, 13)
    return draw_counts(key)


def draw_w2_count(key, part):
    key = jax.random.fold_in(key, 14)
    return draw_counts(key)


def block_levels(rng, dims, cuts, low, top_value):
    level = 1.0
    for dim, shards_of in cuts:
        steps = jax.random.uniform(jax.random.fold_in(jax.random.fold_in(rng, 6), dim), (shards_of,), jnp.float32, low / len(cuts), top_value / len(cuts))
        level = level * jnp.repeat(jnp.exp(steps), dims[dim] // shards_of).reshape((-1,) + (1,) * (len(dims) - 1 - dim))
    return level


def normal_values(key, extent, spread, most, cuts=(), kind=jnp.bfloat16):
    loudness = block_levels(key, extent, cuts, -0.22, 0.18) if cuts else 1.0
    entries = jax.random.normal(key, extent, jnp.float32) * spread * loudness
    return jnp.minimum(jnp.maximum(entries, -most), most).astype(kind)


def setup_inputs(seed: int = 0) -> dict:
    key_list = jax.random.split(jax.random.key(seed), 9)
    return {
        "tokens": normal_values(key_list[0], (TOKENS, D), 1.0, 6.0, ((0, 32), (1, 16))),
        "w1_blocks": normal_values(key_list[1], (N_ROW, N_COL, NB, BS, BS), (BS * N_ROW * NB // HB) ** -0.5, 0.1875, ((0, 16), (1, 16))),
        "w1_coords": draw_w1_coords(jax.random.fold_in(key_list[8], 71), 0),
        "w1_count": draw_w1_count(jax.random.fold_in(key_list[8], 71), 0),
        "w2_blocks": normal_values(key_list[4], (N_ROW, N_COL, NB, BS, BS), (BS * N_COL * NB // DB) ** -0.5, 0.09375, ((0, 16), (1, 16))),
        "w2_coords": draw_w2_coords(jax.random.fold_in(key_list[8], 71), 0),
        "w2_count": draw_w2_count(jax.random.fold_in(key_list[8], 71), 0),
        "cotangent": normal_values(key_list[7], (TOKENS, D), 1.0, 6.0, ((0, 32), (1, 16))),
    }


HIGH = lax.Precision.HIGHEST


def apply_blocks(source, blocks, source_index, target_index, listed, targets, transpose):
    row_count = source.shape[0]
    pieces = source.reshape(row_count, -1, BS).astype(jnp.float32)
    chosen = jnp.take(pieces, source_index, axis=1)
    weights = blocks.astype(jnp.float32)
    if transpose:
        products = jnp.einsum('mnc,nbc->mnb', chosen, weights, precision=HIGH)
    else:
        products = jnp.einsum('mnb,nbc->mnc', chosen, weights, precision=HIGH)
    valid_slots = (jnp.arange(blocks.shape[0], dtype=jnp.int32) < listed).astype(jnp.float32)
    placement = (target_index[:, None] == jnp.arange(targets, dtype=jnp.int32)[None, :]).astype(jnp.float32)
    placement = placement * valid_slots[:, None]
    placed = jnp.einsum('mnc,nh->mhc', products, placement, precision=HIGH)
    return placed.reshape(row_count, targets * BS)


def block_grads(left, right, left_index, right_index, listed):
    row_count = left.shape[0]
    first = jnp.take(left.reshape(row_count, -1, BS).astype(jnp.float32), left_index, axis=1)
    second = jnp.take(right.reshape(row_count, -1, BS).astype(jnp.float32), right_index, axis=1)
    grads = jnp.einsum('mnb,mnc->nbc', first, second, precision=HIGH)
    valid_slots = (jnp.arange(left_index.shape[0], dtype=jnp.int32) < listed).astype(jnp.float32)
    return grads * valid_slots[:, None, None]


def column_part(whole, index, width):
    return lax.dynamic_slice_in_dim(whole, index * width, width, 1)


def rounded_sum(outer, inner, term, start):
    def step(running, index):
        parts = lax.map(lambda other: term(index, other), jnp.arange(inner, dtype=jnp.int32))
        joined = jnp.moveaxis(parts, 0, 1).reshape(parts.shape[1], -1)
        lowered = lax.optimization_barrier(joined.astype(jnp.bfloat16))
        return running + lowered.astype(jnp.float32), None
    result, unused = lax.scan(step, start, jnp.arange(outer, dtype=jnp.int32))
    return result


def reference(tokens, w1_blocks, w1_coords, w1_count, w2_blocks, w2_coords, w2_count, cotangent):
    width_d = D // N_ROW
    width_f = F // N_COL
    total_rows = tokens.shape[0]

    def pre_term(r, c):
        return apply_blocks(column_part(tokens, r, width_d), w1_blocks[r, c], w1_coords[r, c, :, 0],
                            w1_coords[r, c, :, 1], w1_count[r, c], HB, False)

    preact = rounded_sum(N_ROW, N_COL, pre_term, jnp.zeros((total_rows, F), jnp.float32))
    activation = jax.nn.silu(preact).astype(jnp.bfloat16)

    def out_term(c, r):
        return apply_blocks(column_part(activation, c, width_f), w2_blocks[r, c], w2_coords[r, c, :, 0],
                            w2_coords[r, c, :, 1], w2_count[r, c], DB, False)

    output = rounded_sum(N_COL, N_ROW, out_term, jnp.zeros((total_rows, D), jnp.float32)).astype(jnp.bfloat16)

    def act_term(r, c):
        return apply_blocks(column_part(cotangent, r, width_d), w2_blocks[r, c], w2_coords[r, c, :, 1],
                            w2_coords[r, c, :, 0], w2_count[r, c], HB, True)

    act_grad = rounded_sum(N_ROW, N_COL, act_term, jnp.zeros((total_rows, F), jnp.float32))
    sigmoid_pre = jax.nn.sigmoid(preact)
    pre_grad = (act_grad * sigmoid_pre * (1.0 + preact * (1.0 - sigmoid_pre))).astype(jnp.bfloat16)

    def input_term(c, r):
        return apply_blocks(column_part(pre_grad, c, width_f), w1_blocks[r, c], w1_coords[r, c, :, 1],
                            w1_coords[r, c, :, 0], w1_count[r, c], DB, True)

    input_grad = rounded_sum(N_COL, N_ROW, input_term, jnp.zeros((total_rows, D), jnp.float32)).astype(jnp.bfloat16)

    def grad_tile(left, right, left_index, left_width, right_index, right_width, coords, listed):
        running = jnp.zeros((NB, BS, BS), jnp.float32)
        for group in range(N_TOK):
            left_rows = column_part(left[group * TOK:(group + 1) * TOK], left_index, left_width)
            right_rows = column_part(right[group * TOK:(group + 1) * TOK], right_index, right_width)
            grads = block_grads(left_rows, right_rows, coords[:, 0], coords[:, 1], listed)
            running = running + lax.optimization_barrier(grads.astype(jnp.bfloat16)).astype(jnp.float32)
        return running.astype(jnp.bfloat16)

    def first_tile(r, c):
        return grad_tile(tokens, pre_grad, r, width_d, c, width_f, w1_coords[r, c], w1_count[r, c])

    def second_tile(r, c):
        return grad_tile(activation, cotangent, c, width_f, r, width_d, w2_coords[r, c], w2_count[r, c])

    columns = jnp.arange(N_COL, dtype=jnp.int32)
    w1_grad = lax.map(lambda r: lax.map(lambda c: first_tile(r, c), columns), jnp.arange(N_ROW, dtype=jnp.int32))
    w2_grad = lax.map(lambda r: lax.map(lambda c: second_tile(r, c), columns), jnp.arange(N_ROW, dtype=jnp.int32))
    return (output, input_grad, w1_grad, w2_grad)
```

```python
import functools

import jax
import jax.numpy as jnp
from jax import lax
from jax.experimental import pallas as pl
from jax.experimental.pallas import tpu as pltpu
from jax.sharding import PartitionSpec as P

F = 65536
BS = 128
ROWS = 16
VMEM_BYTES = 12 * 1024 * 1024

VMEM = functools.partial(pl.BlockSpec, memory_space=pltpu.VMEM)
SMEM = functools.partial(pl.BlockSpec, memory_space=pltpu.SMEM)


def call(body, in_specs, out_shapes, scratch=(), flops=0, nbytes=0):
    return pl.pallas_call(
        body,
        in_specs=in_specs,
        out_specs=jax.tree.map(lambda _: VMEM(), out_shapes),
        out_shape=out_shapes,
        scratch_shapes=list(scratch),
        compiler_params=pltpu.CompilerParams(vmem_limit_bytes=VMEM_BYTES),
        cost_estimate=pl.CostEstimate(flops=flops, bytes_accessed=nbytes, transcendentals=0),
    )


def slot_products(rows, blocks, source_index, transpose):
    peers, share, width = rows.shape
    slots = blocks.shape[0]
    dims = (((1,), (1,)), ((), ())) if transpose else (((1,), (0,)), ((), ()))

    def body(index_ref, rows_ref, blocks_ref, out_ref):
        for s in range(slots):
            start = pl.multiple_of(index_ref[s] * BS, BS)
            left = rows_ref[:, :, pl.ds(start, BS)].reshape(peers * share, BS)
            product = lax.dot_general(left, blocks_ref[s], dims, preferred_element_type=jnp.float32)
            out_ref[:, s] = product.astype(jnp.bfloat16).reshape(peers, share, BS)

    return call(
        body,
        [SMEM(), VMEM(), VMEM()],
        jax.ShapeDtypeStruct((peers, slots, share, BS), jnp.bfloat16),
        flops=2 * slots * peers * share * BS * BS,
        nbytes=4 * slots * peers * share * BS,
    )(source_index, rows, blocks)


def add_slots(index_ref, offset, parts_ref, total):
    peers, slots = parts_ref.shape[:2]
    total[...] = jnp.zeros_like(total)

    def step(p, carry):
        for s in range(slots):
            target = index_ref[p, offset + s]
            total[target] = total[target] + parts_ref[p, s].astype(jnp.float32)
        return carry

    lax.fori_loop(0, peers, step, 0)


def pick_slots(index_ref, offset, source, out_ref):
    peers, slots = out_ref.shape[:2]

    def step(p, carry):
        for s in range(slots):
            out_ref[p, s] = source[index_ref[p, offset + s]]
        return carry

    lax.fori_loop(0, peers, step, 0)


def activate(parts, index, hidden_blocks):
    peers, slots, share, width = parts.shape

    def body(index_ref, parts_ref, pre_ref, out_ref, total, source):
        add_slots(index_ref, 0, parts_ref, total)
        pre = total[:hidden_blocks]
        pre_ref[...] = pre
        source[:hidden_blocks] = (pre * (1.0 / (1.0 + jnp.exp(-pre)))).astype(jnp.bfloat16)
        source[hidden_blocks:] = jnp.zeros((1, share, width), jnp.bfloat16)
        pick_slots(index_ref, 64, source, out_ref)

    return call(
        body,
        [SMEM(), VMEM()],
        (
            jax.ShapeDtypeStruct((hidden_blocks, share, width), jnp.float32),
            jax.ShapeDtypeStruct(parts.shape, jnp.bfloat16),
        ),
        scratch=[
            pltpu.VMEM((hidden_blocks + 1, share, width), jnp.float32),
            pltpu.VMEM((hidden_blocks + 1, share, width), jnp.bfloat16),
        ],
        flops=4 * parts.size,
        nbytes=6 * parts.size,
    )(index, parts)


def pre_gradient(parts, pre, index):
    peers, slots, share, width = parts.shape
    hidden_blocks = pre.shape[0]

    def body(index_ref, parts_ref, pre_ref, out_ref, total, source):
        add_slots(index_ref, 64, parts_ref, total)
        pre = pre_ref[...]
        gate = 1.0 / (1.0 + jnp.exp(-pre))
        grad = total[:hidden_blocks] * gate * (1.0 + pre * (1.0 - gate))
        source[:hidden_blocks] = grad.astype(jnp.bfloat16)
        source[hidden_blocks:] = jnp.zeros((1, share, width), jnp.bfloat16)
        pick_slots(index_ref, 0, source, out_ref)

    return call(
        body,
        [SMEM(), VMEM(), VMEM()],
        jax.ShapeDtypeStruct(parts.shape, jnp.bfloat16),
        scratch=[
            pltpu.VMEM((hidden_blocks + 1, share, width), jnp.float32),
            pltpu.VMEM((hidden_blocks + 1, share, width), jnp.bfloat16),
        ],
        flops=4 * parts.size,
        nbytes=6 * parts.size,
    )(index, parts, pre)


def feature_sums(slots_in, blocks, target_index, feature_blocks, transpose):
    peers, slots, share, width = slots_in.shape
    dims = (((1,), (1,)), ((), ())) if transpose else (((1,), (0,)), ((), ()))

    def body(index_ref, in_ref, blocks_ref, out_ref, total):
        total[...] = jnp.zeros_like(total)
        for s in range(slots):
            left = in_ref[:, s].reshape(peers * share, width)
            product = lax.dot_general(left, blocks_ref[s], dims, preferred_element_type=jnp.float32)
            target = index_ref[s]
            total[target] = total[target] + product
        for k in range(feature_blocks):
            out_ref[:, k] = total[k].astype(jnp.bfloat16).reshape(peers, share, width)

    return call(
        body,
        [SMEM(), VMEM(), VMEM()],
        jax.ShapeDtypeStruct((peers, feature_blocks, share, width), jnp.bfloat16),
        scratch=[pltpu.VMEM((feature_blocks, peers * share, width), jnp.float32)],
        flops=2 * slots_in.size * BS,
        nbytes=4 * slots_in.size,
    )(target_index, slots_in, blocks)


def block_grads(rows, slots_in, feature_index, rows_first):
    peers, slots, share, width = slots_in.shape
    dims = (((0,), (0,)), ((), ()))

    def body(index_ref, rows_ref, in_ref, out_ref):
        for s in range(slots):
            start = pl.multiple_of(index_ref[s] * BS, BS)
            feature = rows_ref[:, :, pl.ds(start, BS)].reshape(peers * share, BS)
            hidden = in_ref[:, s].reshape(peers * share, width)
            pair = (feature, hidden) if rows_first else (hidden, feature)
            grad = lax.dot_general(*pair, dims, preferred_element_type=jnp.float32)
            out_ref[s] = grad.astype(jnp.bfloat16)

    return call(
        body,
        [SMEM(), VMEM(), VMEM()],
        jax.ShapeDtypeStruct((slots, BS, BS), jnp.bfloat16),
        flops=2 * slots_in.size * BS,
        nbytes=4 * slots_in.size,
    )(feature_index, rows, slots_in)


def owner_sum(parts):
    peers, feature_blocks, share, width = parts.shape

    def body(parts_ref, out_ref):
        for k in range(feature_blocks):
            total = parts_ref[0, k].astype(jnp.float32)
            for c in range(1, peers):
                total = total + parts_ref[c, k].astype(jnp.float32)
            out_ref[:, k * width : (k + 1) * width] = total.astype(jnp.bfloat16)

    return call(
        body,
        [VMEM()],
        jax.ShapeDtypeStruct((share, feature_blocks * width), jnp.bfloat16),
        flops=parts.size,
        nbytes=2 * parts.size,
    )(parts)


def swap(parts, axis):
    return lax.all_to_all(parts, axis, split_axis=0, concat_axis=0, tiled=True)


def gather_tokens(share):
    peers = lax.axis_size("col")
    return swap(jnp.broadcast_to(share[None], (peers,) + share.shape), "col")


def add_groups(grad):
    other = lax.ppermute(grad, "tok", [(0, 1), (1, 0)])
    total = grad.astype(jnp.float32) + other.astype(jnp.float32)
    return total.astype(jnp.bfloat16)[None, None]


def on_device(tokens, w1_blocks, w1_coords, w1_count, w2_blocks, w2_coords, w2_count, cotangent):
    first_blocks, second_blocks = w1_blocks[0, 0], w2_blocks[0, 0]
    first_coords, second_coords = w1_coords[0, 0], w2_coords[0, 0]
    slots = first_blocks.shape[0]
    feature_blocks = tokens.shape[1] // BS
    hidden_blocks = F // lax.axis_size("col") // BS

    live = jnp.arange(slots, dtype=jnp.int32)
    first_hidden = jnp.where(live < w1_count[0, 0], first_coords[:, 1], hidden_blocks)
    second_hidden = jnp.where(live < w2_count[0, 0], second_coords[:, 0], hidden_blocks)
    own = jnp.concatenate(
        [jnp.pad(first_hidden, (0, 64 - slots)), jnp.pad(second_hidden, (0, 64 - slots))]
    )
    rows = lax.axis_size("row")
    index = swap(jnp.broadcast_to(own[None], (rows, 128)), "row")
    first_feature, second_feature = first_coords[:, 0], second_coords[:, 1]

    token_rows = gather_tokens(tokens)
    cotan_rows = gather_tokens(cotangent)
    pre_parts = swap(slot_products(token_rows, first_blocks, first_feature, False), "row")
    act_parts = swap(slot_products(cotan_rows, second_blocks, second_feature, True), "row")
    pre, act_send = activate(pre_parts, index, hidden_blocks)
    act_slots = swap(act_send, "row")
    grad_slots = swap(pre_gradient(act_parts, pre, index), "row")
    out_parts = swap(
        feature_sums(act_slots, second_blocks, second_feature, feature_blocks, False), "col"
    )
    in_parts = swap(
        feature_sums(grad_slots, first_blocks, first_feature, feature_blocks, True), "col"
    )
    second_grad = add_groups(block_grads(cotan_rows, act_slots, second_feature, False))
    first_grad = add_groups(block_grads(token_rows, grad_slots, first_feature, True))
    return owner_sum(out_parts), owner_sum(in_parts), first_grad, second_grad


def solution(mesh):
    placed = (
        P(("tok", "col"), "row"),
        P("row", "col", None, None, None),
        P("row", "col", None, None),
        P("row", "col"),
        P("row", "col", None, None, None),
        P("row", "col", None, None),
        P("row", "col"),
        P(("tok", "col"), "row"),
    )
    return jax.shard_map(
        on_device,
        mesh=mesh,
        in_specs=placed,
        out_specs=(
            P(("tok", "col"), "row"),
            P(("tok", "col"), "row"),
            P("row", "col", None, None, None),
            P("row", "col", None, None, None),
        ),
        check_vma=False,
    )
```

```python
import functools

import jax
import jax.numpy as jnp
from jax import lax
from jax.experimental import pallas as pl
from jax.experimental.pallas import tpu as pltpu
from jax.sharding import PartitionSpec as P

F = 65536
BS = 128
ROWS = 16
VMEM_BYTES = 12 * 1024 * 1024

VMEM = functools.partial(pl.BlockSpec, memory_space=pltpu.VMEM)
SMEM = functools.partial(pl.BlockSpec, memory_space=pltpu.SMEM)


def call(body, in_specs, out_shapes, scratch=(), flops=0, nbytes=0):
    return pl.pallas_call(
        body,
        in_specs=in_specs,
        out_specs=jax.tree.map(lambda _: VMEM(), out_shapes),
        out_shape=out_shapes,
        scratch_shapes=list(scratch),
        compiler_params=pltpu.CompilerParams(vmem_limit_bytes=VMEM_BYTES),
        cost_estimate=pl.CostEstimate(flops=flops, bytes_accessed=nbytes, transcendentals=0),
    )


def product_dims(transpose):
    return (((1,), (1,)), ((), ())) if transpose else (((1,), (0,)), ((), ()))


def slot_products(tokens, cotangent, first, second, first_feature, second_feature, table):
    peers, share, width = tokens.shape
    slots = first.shape[0]

    def body(i1_ref, i2_ref, x_ref, g_ref, w1_ref, w2_ref, table_ref, out_ref):
        for base, index_ref, rows_ref, blocks_ref in (
            (0, i1_ref, x_ref, w1_ref),
            (slots, i2_ref, g_ref, w2_ref),
        ):
            for s in range(slots):
                start = pl.multiple_of(index_ref[s] * BS, BS)
                left = rows_ref[:, :, pl.ds(start, BS)].reshape(peers * share, BS)
                product = lax.dot_general(
                    left, blocks_ref[s], product_dims(base > 0), preferred_element_type=jnp.float32
                )
                out_ref[:, base + s] = product.astype(jnp.bfloat16).reshape(peers, share, BS)
        for p in range(peers):
            out_ref[p, 2 * slots] = table_ref[...]

    return call(
        body,
        [SMEM()] * 2 + [VMEM()] * 5,
        jax.ShapeDtypeStruct((peers, 2 * slots + 1, share, BS), jnp.bfloat16),
        flops=4 * slots * peers * share * BS * BS,
        nbytes=8 * slots * peers * share * BS,
    )(first_feature, second_feature, tokens, cotangent, first, second, table)


def hidden_step(parts, hidden_blocks):
    peers, width = parts.shape[0], parts.shape[3]
    slots = parts.shape[1] // 2
    share = parts.shape[2]

    def body(parts_ref, out_ref, pre, grad, act_blocks, grad_blocks, table, index, sem):
        row = lax.broadcasted_iota(jnp.int32, (peers, width), 0)
        lines = jnp.zeros((peers, width), jnp.float32)
        for p in range(peers):
            lines = jnp.where(row == p, parts_ref[p, 2 * slots].astype(jnp.float32), lines)
        table[...] = lines.astype(jnp.int32)
        copy = pltpu.make_async_copy(table, index, sem)
        copy.start()
        pre[...] = jnp.zeros_like(pre)
        grad[...] = jnp.zeros_like(grad)
        act_blocks[hidden_blocks:] = jnp.zeros((1, share, width), jnp.bfloat16)
        grad_blocks[hidden_blocks:] = jnp.zeros((1, share, width), jnp.bfloat16)
        copy.wait()

        def add(p, carry):
            for s in range(slots):
                i, j = index[p, s], index[p, 64 + s]
                pre[i] = pre[i] + parts_ref[p, s].astype(jnp.float32)
                grad[j] = grad[j] + parts_ref[p, slots + s].astype(jnp.float32)
            return carry

        lax.fori_loop(0, peers, add, 0)

        def point(h, carry):
            value = pre[h]
            gate = 1.0 / (1.0 + jnp.exp(-value))
            act_blocks[h] = (value * gate).astype(jnp.bfloat16)
            grad_blocks[h] = (grad[h] * gate * (1.0 + value * (1.0 - gate))).astype(jnp.bfloat16)
            return carry

        lax.fori_loop(0, hidden_blocks, point, 0, unroll=8)

        def pick(p, carry):
            for s in range(slots):
                out_ref[p, s] = act_blocks[index[p, 64 + s]]
                out_ref[p, slots + s] = grad_blocks[index[p, s]]
            return carry

        lax.fori_loop(0, peers, pick, 0)

    return call(
        body,
        [VMEM()],
        jax.ShapeDtypeStruct((peers, 2 * slots, share, width), jnp.bfloat16),
        scratch=[
            pltpu.VMEM((hidden_blocks + 1, share, width), jnp.float32),
            pltpu.VMEM((hidden_blocks + 1, share, width), jnp.float32),
            pltpu.VMEM((hidden_blocks + 1, share, width), jnp.bfloat16),
            pltpu.VMEM((hidden_blocks + 1, share, width), jnp.bfloat16),
            pltpu.VMEM((peers, width), jnp.int32),
            pltpu.SMEM((peers, width), jnp.int32),
            pltpu.SemaphoreType.DMA,
        ],
        flops=4 * parts.size,
        nbytes=6 * parts.size,
    )(parts)


def feature_sums(slots_in, first, second, first_feature, second_feature, feature_blocks):
    peers, both, share, width = slots_in.shape
    slots = both // 2

    def body(i1_ref, i2_ref, in_ref, w1_ref, w2_ref, out_ref, total):
        for base, index_ref, blocks_ref in ((0, i2_ref, w2_ref), (slots, i1_ref, w1_ref)):
            total[...] = jnp.zeros_like(total)
            for s in range(slots):
                left = in_ref[:, base + s].reshape(peers * share, width)
                product = lax.dot_general(
                    left, blocks_ref[s], product_dims(base > 0), preferred_element_type=jnp.float32
                )
                target = index_ref[s]
                total[target] = total[target] + product
            place = feature_blocks if base else 0
            for k in range(feature_blocks):
                out_ref[:, place + k] = total[k].astype(jnp.bfloat16).reshape(peers, share, width)

    return call(
        body,
        [SMEM()] * 2 + [VMEM()] * 3,
        jax.ShapeDtypeStruct((peers, 2 * feature_blocks, share, width), jnp.bfloat16),
        scratch=[pltpu.VMEM((feature_blocks, peers * share, width), jnp.float32)],
        flops=2 * slots_in.size * BS,
        nbytes=4 * slots_in.size,
    )(first_feature, second_feature, slots_in, first, second)


def block_grads(tokens, cotangent, slots_in, first_feature, second_feature):
    peers, both, share, width = slots_in.shape
    slots = both // 2
    dims = (((0,), (0,)), ((), ()))

    def body(i1_ref, i2_ref, x_ref, g_ref, in_ref, out_ref):
        for s in range(slots):
            start = pl.multiple_of(i1_ref[s] * BS, BS)
            feature = x_ref[:, :, pl.ds(start, BS)].reshape(peers * share, BS)
            hidden = in_ref[:, slots + s].reshape(peers * share, width)
            grad = lax.dot_general(feature, hidden, dims, preferred_element_type=jnp.float32)
            out_ref[s] = grad.astype(jnp.bfloat16)
        for s in range(slots):
            start = pl.multiple_of(i2_ref[s] * BS, BS)
            feature = g_ref[:, :, pl.ds(start, BS)].reshape(peers * share, BS)
            hidden = in_ref[:, s].reshape(peers * share, width)
            grad = lax.dot_general(hidden, feature, dims, preferred_element_type=jnp.float32)
            out_ref[slots + s] = grad.astype(jnp.bfloat16)

    return call(
        body,
        [SMEM()] * 2 + [VMEM()] * 3,
        jax.ShapeDtypeStruct((both, BS, BS), jnp.bfloat16),
        flops=2 * slots_in.size * BS,
        nbytes=4 * slots_in.size,
    )(first_feature, second_feature, tokens, cotangent, slots_in)


def owner_sums(parts):
    peers, both, share, width = parts.shape
    feature_blocks = both // 2

    def body(parts_ref, out_ref, in_ref):
        for k in range(both):
            total = parts_ref[0, k].astype(jnp.float32)
            for c in range(1, peers):
                total = total + parts_ref[c, k].astype(jnp.float32)
            target, place = (out_ref, k) if k < feature_blocks else (in_ref, k - feature_blocks)
            target[:, place * width : (place + 1) * width] = total.astype(jnp.bfloat16)

    shape = jax.ShapeDtypeStruct((share, feature_blocks * width), jnp.bfloat16)
    return call(body, [VMEM()], (shape, shape), flops=parts.size, nbytes=2 * parts.size)(parts)


def swap(parts, axis):
    return lax.all_to_all(parts, axis, split_axis=0, concat_axis=0, tiled=True)


def on_device(tokens, w1_blocks, w1_coords, w1_count, w2_blocks, w2_coords, w2_count, cotangent):
    first, second = w1_blocks[0, 0], w2_blocks[0, 0]
    first_coords, second_coords = w1_coords[0, 0], w2_coords[0, 0]
    slots = first.shape[0]
    feature_blocks = tokens.shape[1] // BS
    hidden_blocks = F // lax.axis_size("col") // BS
    first_feature, second_feature = first_coords[:, 0], second_coords[:, 1]

    live = jnp.arange(slots, dtype=jnp.int32)
    first_hidden = jnp.where(live < w1_count[0, 0], first_coords[:, 1], hidden_blocks)
    second_hidden = jnp.where(live < w2_count[0, 0], second_coords[:, 0], hidden_blocks)
    line = jnp.pad(first_hidden, (0, BS - slots)) + jnp.pad(second_hidden, (64, 64 - slots))
    table = jnp.broadcast_to(line.astype(jnp.bfloat16), (tokens.shape[0], BS))

    peers = lax.axis_size("col")
    cotan_rows = swap(jnp.broadcast_to(cotangent[None], (peers,) + cotangent.shape), "col")
    token_rows = lax.all_gather(tokens, "col", axis=0, tiled=True).reshape(cotan_rows.shape)
    parts = swap(
        slot_products(token_rows, cotan_rows, first, second, first_feature, second_feature, table),
        "row",
    )
    slots_in = swap(hidden_step(parts, hidden_blocks), "row")
    sums = swap(
        feature_sums(slots_in, first, second, first_feature, second_feature, feature_blocks), "col"
    )
    grads = block_grads(token_rows, cotan_rows, slots_in, first_feature, second_feature)
    others = lax.ppermute(grads, "tok", [(0, 1), (1, 0)])
    grads = (grads.astype(jnp.float32) + others.astype(jnp.float32)).astype(jnp.bfloat16)
    output, input_grad = owner_sums(sums)
    return output, input_grad, grads[None, None, :slots], grads[None, None, slots:]


def solution(mesh):
    placed = (
        P(("tok", "col"), "row"),
        P("row", "col", None, None, None),
        P("row", "col", None, None),
        P("row", "col"),
        P("row", "col", None, None, None),
        P("row", "col", None, None),
        P("row", "col"),
        P(("tok", "col"), "row"),
    )
    return jax.shard_map(
        on_device,
        mesh=mesh,
        in_specs=placed,
        out_specs=(
            P(("tok", "col"), "row"),
            P(("tok", "col"), "row"),
            P("row", "col", None, None, None),
            P("row", "col", None, None, None),
        ),
        check_vma=False,
    )
```

```python
import functools

import jax
import jax.numpy as jnp
from jax import lax
from jax.experimental import pallas as pl
from jax.experimental.pallas import tpu as pltpu
from jax.sharding import PartitionSpec as P

BS = 128
FEATURE = 8
HIDDEN = 32
VMEM_BYTES = 12 * 1024 * 1024

VMEM = functools.partial(pl.BlockSpec, memory_space=pltpu.VMEM)
SMEM = functools.partial(pl.BlockSpec, memory_space=pltpu.SMEM)


def call(body, in_specs, out_shapes, scratch=(), flops=0, nbytes=0):
    return pl.pallas_call(
        body,
        in_specs=in_specs,
        out_specs=jax.tree.map(lambda _: VMEM(), out_shapes),
        out_shape=out_shapes,
        scratch_shapes=list(scratch),
        compiler_params=pltpu.CompilerParams(vmem_limit_bytes=VMEM_BYTES),
        cost_estimate=pl.CostEstimate(flops=flops, bytes_accessed=nbytes, transcendentals=0),
    )


def product_dims(transpose):
    return (((1,), (1,)), ((), ())) if transpose else (((1,), (0,)), ((), ()))


def slot_products(rows, first, second, first_coords, second_coords, first_count, second_count):
    peers, both, share, width = rows.shape
    slots = first.shape[0]

    def body(c1_ref, c2_ref, n1_ref, n2_ref, rows_ref, w1_ref, w2_ref, out_ref):
        lane = lax.broadcasted_iota(jnp.int32, (share, BS), 1)
        table = jnp.zeros((share, BS), jnp.int32)
        for s in range(slots):
            i = jnp.where(s < n1_ref[0, 0], c1_ref[1, s], HIDDEN)
            j = jnp.where(s < n2_ref[0, 0], c2_ref[0, s], HIDDEN)
            table = jnp.where(lane == s, i, jnp.where(lane == 64 + s, j, table))
        table = table.astype(jnp.float32).astype(jnp.bfloat16)
        for p in range(peers):
            out_ref[p, 2 * slots] = table
        for base, line, index_ref, blocks_ref in ((0, 0, c1_ref, w1_ref), (slots, 1, c2_ref, w2_ref)):
            for s in range(slots):
                start = pl.multiple_of(index_ref[line, s] * BS, BS)
                left = rows_ref[:, line, :, pl.ds(start, BS)].reshape(peers * share, BS)
                product = lax.dot_general(
                    left, blocks_ref[s], product_dims(line > 0), preferred_element_type=jnp.float32
                )
                out_ref[:, base + s] = product.astype(jnp.bfloat16).reshape(peers, share, BS)

    return call(
        body,
        [SMEM()] * 4 + [VMEM()] * 3,
        jax.ShapeDtypeStruct((peers, 2 * slots + 1, share, BS), jnp.bfloat16),
        flops=4 * slots * peers * share * BS * BS,
        nbytes=8 * slots * peers * share * BS,
    )(first_coords, second_coords, first_count, second_count, rows, first, second)


def hidden_step(parts):
    peers, width = parts.shape[0], parts.shape[3]
    slots = parts.shape[1] // 2
    share = parts.shape[2]
    hidden_blocks = HIDDEN

    def body(parts_ref, out_ref, pre, grad, act_blocks, grad_blocks, table, index, sem):
        row = lax.broadcasted_iota(jnp.int32, (peers, width), 0)
        lines = jnp.zeros((peers, width), jnp.float32)
        for p in range(peers):
            lines = jnp.where(row == p, parts_ref[p, 2 * slots].astype(jnp.float32), lines)
        table[...] = lines.astype(jnp.int32)
        copy = pltpu.make_async_copy(table, index, sem)
        copy.start()
        pre[...] = jnp.zeros_like(pre)
        grad[...] = jnp.zeros_like(grad)
        act_blocks[hidden_blocks:] = jnp.zeros((1, share, width), jnp.bfloat16)
        grad_blocks[hidden_blocks:] = jnp.zeros((1, share, width), jnp.bfloat16)
        copy.wait()

        def add(p, carry):
            for s in range(slots):
                i, j = index[p, s], index[p, 64 + s]
                pre[i] = pre[i] + parts_ref[p, s].astype(jnp.float32)
                grad[j] = grad[j] + parts_ref[p, slots + s].astype(jnp.float32)
            return carry

        lax.fori_loop(0, peers, add, 0)

        def point(h, carry):
            value = pre[h]
            gate = 1.0 / (1.0 + jnp.exp(-value))
            act_blocks[h] = (value * gate).astype(jnp.bfloat16)
            grad_blocks[h] = (grad[h] * gate * (1.0 + value * (1.0 - gate))).astype(jnp.bfloat16)
            return carry

        lax.fori_loop(0, hidden_blocks, point, 0, unroll=8)

        def pick(p, carry):
            for s in range(slots):
                out_ref[p, s] = act_blocks[index[p, 64 + s]]
                out_ref[p, slots + s] = grad_blocks[index[p, s]]
            return carry

        lax.fori_loop(0, peers, pick, 0)

    return call(
        body,
        [VMEM()],
        jax.ShapeDtypeStruct((peers, 2 * slots, share, width), jnp.bfloat16),
        scratch=[
            pltpu.VMEM((hidden_blocks + 1, share, width), jnp.float32),
            pltpu.VMEM((hidden_blocks + 1, share, width), jnp.float32),
            pltpu.VMEM((hidden_blocks + 1, share, width), jnp.bfloat16),
            pltpu.VMEM((hidden_blocks + 1, share, width), jnp.bfloat16),
            pltpu.VMEM((peers, width), jnp.int32),
            pltpu.SMEM((peers, width), jnp.int32),
            pltpu.SemaphoreType.DMA,
        ],
        flops=4 * parts.size,
        nbytes=6 * parts.size,
    )(parts)


def feature_sums(slots_in, first, second, first_coords, second_coords):
    peers, both, share, width = slots_in.shape
    slots = both // 2

    def body(c1_ref, c2_ref, in_ref, w1_ref, w2_ref, out_ref, total):
        for base, line, index_ref, blocks_ref in ((0, 1, c2_ref, w2_ref), (slots, 0, c1_ref, w1_ref)):
            total[...] = jnp.zeros_like(total)
            for s in range(slots):
                left = in_ref[:, base + s].reshape(peers * share, width)
                product = lax.dot_general(
                    left, blocks_ref[s], product_dims(base > 0), preferred_element_type=jnp.float32
                )
                target = index_ref[line, s]
                total[target] = total[target] + product
            place = FEATURE if base else 0
            for k in range(FEATURE):
                out_ref[:, place + k] = total[k].astype(jnp.bfloat16).reshape(peers, share, width)

    return call(
        body,
        [SMEM()] * 2 + [VMEM()] * 3,
        jax.ShapeDtypeStruct((peers, 2 * FEATURE, share, width), jnp.bfloat16),
        scratch=[pltpu.VMEM((FEATURE, peers * share, width), jnp.float32)],
        flops=2 * slots_in.size * BS,
        nbytes=4 * slots_in.size,
    )(first_coords, second_coords, slots_in, first, second)


def block_grads(rows, slots_in, first_coords, second_coords):
    peers, both, share, width = slots_in.shape
    slots = both // 2
    dims = (((0,), (0,)), ((), ()))

    def body(c1_ref, c2_ref, rows_ref, in_ref, out_ref):
        for s in range(slots):
            start = pl.multiple_of(c1_ref[0, s] * BS, BS)
            feature = rows_ref[:, 0, :, pl.ds(start, BS)].reshape(peers * share, BS)
            hidden = in_ref[:, slots + s].reshape(peers * share, width)
            grad = lax.dot_general(feature, hidden, dims, preferred_element_type=jnp.float32)
            out_ref[s] = grad.astype(jnp.bfloat16)
        for s in range(slots):
            start = pl.multiple_of(c2_ref[1, s] * BS, BS)
            feature = rows_ref[:, 1, :, pl.ds(start, BS)].reshape(peers * share, BS)
            hidden = in_ref[:, s].reshape(peers * share, width)
            grad = lax.dot_general(hidden, feature, dims, preferred_element_type=jnp.float32)
            out_ref[slots + s] = grad.astype(jnp.bfloat16)

    return call(
        body,
        [SMEM()] * 2 + [VMEM()] * 2,
        jax.ShapeDtypeStruct((both, BS, BS), jnp.bfloat16),
        flops=2 * slots_in.size * BS,
        nbytes=4 * slots_in.size,
    )(first_coords, second_coords, rows, slots_in)


def final_sums(parts, grads, others):
    peers, both, share, width = parts.shape
    slots = grads.shape[0] // 2

    def body(parts_ref, grads_ref, others_ref, out_ref, in_ref, w1_ref, w2_ref):
        for s in range(2 * slots):
            total = grads_ref[s].astype(jnp.float32) + others_ref[s].astype(jnp.float32)
            target = w1_ref if s < slots else w2_ref
            target[0, 0, s % slots] = total.astype(jnp.bfloat16)
        for k in range(both):
            total = parts_ref[0, k].astype(jnp.float32)
            for c in range(1, peers):
                total = total + parts_ref[c, k].astype(jnp.float32)
            target, place = (out_ref, k) if k < FEATURE else (in_ref, k - FEATURE)
            target[:, place * width : (place + 1) * width] = total.astype(jnp.bfloat16)

    row = jax.ShapeDtypeStruct((share, FEATURE * width), jnp.bfloat16)
    grad = jax.ShapeDtypeStruct((1, 1, slots, BS, BS), jnp.bfloat16)
    return call(
        body, [VMEM()] * 3, (row, row, grad, grad), flops=parts.size, nbytes=2 * parts.size
    )(parts, grads, others)


def swap(parts, axis):
    return lax.all_to_all(parts, axis, split_axis=0, concat_axis=0, tiled=True)


def on_device(tokens, w1_blocks, w1_coords, w1_count, w2_blocks, w2_coords, w2_count, cotangent):
    first, second = w1_blocks[0, 0], w2_blocks[0, 0]
    first_coords, second_coords = w1_coords[0, 0].T, w2_coords[0, 0].T
    peers = lax.axis_size("col")
    rows = jnp.stack([tokens, cotangent])
    rows = swap(jnp.broadcast_to(rows[None], (peers,) + rows.shape), "col")
    parts = swap(
        slot_products(rows, first, second, first_coords, second_coords, w1_count, w2_count), "row"
    )
    slots_in = swap(hidden_step(parts), "row")
    grads = block_grads(rows, slots_in, first_coords, second_coords)
    grads, slots_in = lax.optimization_barrier((grads, slots_in))
    others = lax.ppermute(grads, "tok", [(0, 1), (1, 0)])
    sums = swap(feature_sums(slots_in, first, second, first_coords, second_coords), "col")
    return final_sums(sums, grads, others)


def solution(mesh):
    placed = (
        P(("tok", "col"), "row"),
        P("row", "col", None, None, None),
        P("row", "col", None, None),
        P("row", "col"),
        P("row", "col", None, None, None),
        P("row", "col", None, None),
        P("row", "col"),
        P(("tok", "col"), "row"),
    )
    return jax.shard_map(
        on_device,
        mesh=mesh,
        in_specs=placed,
        out_specs=(
            P(("tok", "col"), "row"),
            P(("tok", "col"), "row"),
            P("row", "col", None, None, None),
            P("row", "col", None, None, None),
        ),
        check_vma=False,
    )
```

```python
import functools

import jax
import jax.numpy as jnp
from jax import lax
from jax.experimental import pallas as pl
from jax.experimental.pallas import tpu as pltpu
from jax.sharding import PartitionSpec as P

BS = 128
FEATURE = 8
HIDDEN = 32
NEAR = 4
VMEM_BYTES = 12 * 1024 * 1024

VMEM = functools.partial(pl.BlockSpec, memory_space=pltpu.VMEM)
SMEM = functools.partial(pl.BlockSpec, memory_space=pltpu.SMEM)


def call(body, in_specs, out_shapes, scratch=(), flops=0, nbytes=0):
    return pl.pallas_call(
        body,
        in_specs=in_specs,
        out_specs=jax.tree.map(lambda _: VMEM(), out_shapes),
        out_shape=out_shapes,
        scratch_shapes=list(scratch),
        compiler_params=pltpu.CompilerParams(vmem_limit_bytes=VMEM_BYTES),
        cost_estimate=pl.CostEstimate(flops=flops, bytes_accessed=nbytes, transcendentals=0),
    )


def product_dims(transpose):
    return (((1,), (1,)), ((), ())) if transpose else (((1,), (0,)), ((), ()))


def block_column(rows_refs, line, index):
    start = pl.multiple_of(index * BS, BS)
    parts = [ref[:, line, :, pl.ds(start, BS)] for ref in rows_refs]
    return jnp.concatenate(parts, axis=0).reshape(-1, BS)


def slot_products(rows, first, second, first_coords, second_coords, first_count, second_count):
    group, both, share, width = rows[0].shape
    peers = group * len(rows)
    slots = first.shape[0]

    def body(c1_ref, c2_ref, n1_ref, n2_ref, *refs):
        rows_refs, (w1_ref, w2_ref, out_ref) = refs[: len(rows)], refs[len(rows) :]
        lane = lax.broadcasted_iota(jnp.int32, (share, BS), 1)
        table = jnp.zeros((share, BS), jnp.int32)
        for s in range(slots):
            i = jnp.where(s < n1_ref[0, 0], c1_ref[1, s], HIDDEN)
            j = jnp.where(s < n2_ref[0, 0], c2_ref[0, s], HIDDEN)
            table = jnp.where(lane == s, i, jnp.where(lane == 64 + s, j, table))
        table = table.astype(jnp.float32).astype(jnp.bfloat16)
        for p in range(peers):
            out_ref[p, 2 * slots] = table
        for base, line, index_ref, blocks_ref in ((0, 0, c1_ref, w1_ref), (slots, 1, c2_ref, w2_ref)):
            for s in range(slots):
                left = block_column(rows_refs, line, index_ref[line, s])
                product = lax.dot_general(
                    left, blocks_ref[s], product_dims(line > 0), preferred_element_type=jnp.float32
                )
                out_ref[:, base + s] = product.astype(jnp.bfloat16).reshape(peers, share, BS)

    return call(
        body,
        [SMEM()] * 4 + [VMEM()] * (len(rows) + 2),
        jax.ShapeDtypeStruct((peers, 2 * slots + 1, share, BS), jnp.bfloat16),
        flops=4 * slots * peers * share * BS * BS,
        nbytes=8 * slots * peers * share * BS,
    )(first_coords, second_coords, first_count, second_count, *rows, first, second)


def hidden_step(parts):
    peers, width = parts.shape[0], parts.shape[3]
    slots = parts.shape[1] // 2
    share = parts.shape[2]
    hidden_blocks = HIDDEN

    def body(parts_ref, out_ref, pre, grad, act_blocks, grad_blocks, table, index, sem):
        row = lax.broadcasted_iota(jnp.int32, (peers, width), 0)
        lines = jnp.zeros((peers, width), jnp.float32)
        for p in range(peers):
            lines = jnp.where(row == p, parts_ref[p, 2 * slots].astype(jnp.float32), lines)
        table[...] = lines.astype(jnp.int32)
        copy = pltpu.make_async_copy(table, index, sem)
        copy.start()
        pre[...] = jnp.zeros_like(pre)
        grad[...] = jnp.zeros_like(grad)
        act_blocks[hidden_blocks:] = jnp.zeros((1, share, width), jnp.bfloat16)
        grad_blocks[hidden_blocks:] = jnp.zeros((1, share, width), jnp.bfloat16)
        copy.wait()

        def add(p, carry):
            for s in range(slots):
                i, j = index[p, s], index[p, 64 + s]
                pre[i] = pre[i] + parts_ref[p, s].astype(jnp.float32)
                grad[j] = grad[j] + parts_ref[p, slots + s].astype(jnp.float32)
            return carry

        lax.fori_loop(0, peers, add, 0)

        def point(h, carry):
            value = pre[h]
            gate = 1.0 / (1.0 + jnp.exp(-value))
            act_blocks[h] = (value * gate).astype(jnp.bfloat16)
            grad_blocks[h] = (grad[h] * gate * (1.0 + value * (1.0 - gate))).astype(jnp.bfloat16)
            return carry

        lax.fori_loop(0, hidden_blocks, point, 0, unroll=8)

        def pick(p, carry):
            for s in range(slots):
                out_ref[p, s] = act_blocks[index[p, 64 + s]]
                out_ref[p, slots + s] = grad_blocks[index[p, s]]
            return carry

        lax.fori_loop(0, peers, pick, 0)

    return call(
        body,
        [VMEM()],
        jax.ShapeDtypeStruct((peers, 2 * slots, share, width), jnp.bfloat16),
        scratch=[
            pltpu.VMEM((hidden_blocks + 1, share, width), jnp.float32),
            pltpu.VMEM((hidden_blocks + 1, share, width), jnp.float32),
            pltpu.VMEM((hidden_blocks + 1, share, width), jnp.bfloat16),
            pltpu.VMEM((hidden_blocks + 1, share, width), jnp.bfloat16),
            pltpu.VMEM((peers, width), jnp.int32),
            pltpu.SMEM((peers, width), jnp.int32),
            pltpu.SemaphoreType.DMA,
        ],
        flops=4 * parts.size,
        nbytes=6 * parts.size,
    )(parts)


def feature_sums(slots_in, first, second, first_coords, second_coords):
    peers, both, share, width = slots_in.shape
    slots = both // 2
    group = peers // NEAR

    def body(c1_ref, c2_ref, in_ref, w1_ref, w2_ref, *refs):
        out_refs, total = refs[:NEAR], refs[NEAR]
        for base, line, index_ref, blocks_ref in ((0, 1, c2_ref, w2_ref), (slots, 0, c1_ref, w1_ref)):
            total[...] = jnp.zeros_like(total)
            for s in range(slots):
                left = in_ref[:, base + s].reshape(peers * share, width)
                product = lax.dot_general(
                    left, blocks_ref[s], product_dims(base > 0), preferred_element_type=jnp.float32
                )
                target = index_ref[line, s]
                total[target] = total[target] + product
            place = FEATURE if base else 0
            for k in range(FEATURE):
                value = total[k].astype(jnp.bfloat16).reshape(NEAR, group, share, width)
                for n in range(NEAR):
                    out_refs[n][:, place + k] = value[n]

    return call(
        body,
        [SMEM()] * 2 + [VMEM()] * 3,
        (jax.ShapeDtypeStruct((group, 2 * FEATURE, share, width), jnp.bfloat16),) * NEAR,
        scratch=[pltpu.VMEM((FEATURE, peers * share, width), jnp.float32)],
        flops=2 * slots_in.size * BS,
        nbytes=4 * slots_in.size,
    )(first_coords, second_coords, slots_in, first, second)


def block_grads(rows, slots_in, first_coords, second_coords):
    peers, both, share, width = slots_in.shape
    slots = both // 2
    dims = (((0,), (0,)), ((), ()))

    def body(c1_ref, c2_ref, *refs):
        rows_refs, (in_ref, out_ref) = refs[: len(rows)], refs[len(rows) :]
        for s in range(slots):
            feature = block_column(rows_refs, 0, c1_ref[0, s])
            hidden = in_ref[:, slots + s].reshape(peers * share, width)
            grad = lax.dot_general(feature, hidden, dims, preferred_element_type=jnp.float32)
            out_ref[s] = grad.astype(jnp.bfloat16)
        for s in range(slots):
            feature = block_column(rows_refs, 1, c2_ref[1, s])
            hidden = in_ref[:, s].reshape(peers * share, width)
            grad = lax.dot_general(hidden, feature, dims, preferred_element_type=jnp.float32)
            out_ref[slots + s] = grad.astype(jnp.bfloat16)

    return call(
        body,
        [SMEM()] * 2 + [VMEM()] * (len(rows) + 1),
        jax.ShapeDtypeStruct((both, BS, BS), jnp.bfloat16),
        flops=2 * slots_in.size * BS,
        nbytes=4 * slots_in.size,
    )(first_coords, second_coords, *rows, slots_in)


def near_sums(parts, far_place):
    group, blocks, share, width = parts[0].shape

    def body(place_ref, *refs):
        part_refs, out_refs = refs[:NEAR], refs[NEAR:]
        for step in range(group):
            k = lax.rem(place_ref[0] + step, group)

            def add(b, carry):
                total = part_refs[0][k, b].astype(jnp.float32)
                for ref in part_refs[1:]:
                    total = total + ref[k, b].astype(jnp.float32)
                out_refs[step][b] = total.astype(jnp.bfloat16)
                return carry

            lax.fori_loop(0, blocks, add, 0, unroll=True)

    return call(
        body,
        [SMEM()] + [VMEM()] * NEAR,
        (jax.ShapeDtypeStruct((blocks, share, width), jnp.bfloat16),) * group,
        flops=4 * parts[0].size,
        nbytes=8 * parts[0].size,
    )(far_place, *parts)


def final_sums(parts, grads, others):
    both, share, width = parts[0].shape
    slots = grads.shape[0] // 2

    def body(*refs):
        part_refs, refs = refs[: len(parts)], refs[len(parts) :]
        grads_ref, others_ref, out_ref, in_ref, w1_ref, w2_ref = refs
        for s in range(2 * slots):
            total = grads_ref[s].astype(jnp.float32) + others_ref[s].astype(jnp.float32)
            target = w1_ref if s < slots else w2_ref
            target[0, 0, s % slots] = total.astype(jnp.bfloat16)
        for k in range(both):
            total = part_refs[0][k].astype(jnp.float32)
            for ref in part_refs[1:]:
                total = total + ref[k].astype(jnp.float32)
            target, place = (out_ref, k) if k < FEATURE else (in_ref, k - FEATURE)
            target[:, place * width : (place + 1) * width] = total.astype(jnp.bfloat16)

    row = jax.ShapeDtypeStruct((share, FEATURE * width), jnp.bfloat16)
    grad = jax.ShapeDtypeStruct((1, 1, slots, BS, BS), jnp.bfloat16)
    return call(
        body,
        [VMEM()] * (len(parts) + 2),
        (row, row, grad, grad),
        flops=grads.size,
        nbytes=6 * grads.size,
    )(*parts, grads, others)


def swap(parts, axis):
    return lax.all_to_all(parts, axis, split_axis=0, concat_axis=0, tiled=True)


def send_on(value, hops):
    peers = lax.axis_size("col")
    return lax.ppermute(value, "col", [(c, (c + hops) % peers) for c in range(peers)])


def on_device(tokens, w1_blocks, w1_coords, w1_count, w2_blocks, w2_coords, w2_count, cotangent):
    first, second = w1_blocks[0, 0], w2_blocks[0, 0]
    first_coords, second_coords = w1_coords[0, 0].T, w2_coords[0, 0].T
    peers = lax.axis_size("col")
    far = [[c + NEAR * k for k in range(peers // NEAR)] for c in range(NEAR)]
    steps = (0, 1, -1, 2)

    own = lax.all_gather(jnp.stack([tokens, cotangent]), "col", axis_index_groups=far)
    rows = [own] + [send_on(own, -step) for step in steps[1:]]
    parts = swap(
        slot_products(rows, first, second, first_coords, second_coords, w1_count, w2_count), "row"
    )
    slots_in = swap(hidden_step(parts), "row")
    sums = feature_sums(slots_in, first, second, first_coords, second_coords)
    sums = [sums[0]] + [send_on(part, step) for part, step in zip(sums[1:], steps[1:])]
    grads = block_grads(rows, slots_in, first_coords, second_coords)
    others = lax.ppermute(grads, "tok", [(0, 1), (1, 0)])
    sums = near_sums(sums, lax.div(lax.axis_index("col"), NEAR).reshape(1))
    sums = [sums[0]] + [send_on(sums[k], NEAR * k) for k in range(1, peers // NEAR)]
    return final_sums(sums, grads, others)


def solution(mesh):
    placed = (
        P(("tok", "col"), "row"),
        P("row", "col", None, None, None),
        P("row", "col", None, None),
        P("row", "col"),
        P("row", "col", None, None, None),
        P("row", "col", None, None),
        P("row", "col"),
        P(("tok", "col"), "row"),
    )
    return jax.shard_map(
        on_device,
        mesh=mesh,
        in_specs=placed,
        out_specs=(
            P(("tok", "col"), "row"),
            P(("tok", "col"), "row"),
            P("row", "col", None, None, None),
            P("row", "col", None, None, None),
        ),
        check_vma=False,
    )
```

```python
import functools

import jax
import jax.numpy as jnp
from jax import lax
from jax.experimental import pallas as pl
from jax.experimental.pallas import tpu as pltpu
from jax.sharding import PartitionSpec as P

BS = 128
FEATURE = 8
HIDDEN = 32
NEAR = 4
STEPS = (0, 1, -1, 2, -2)
PLACES = (4, 4, 4, 2, 2)
VMEM_BYTES = 12 * 1024 * 1024

VMEM = functools.partial(pl.BlockSpec, memory_space=pltpu.VMEM)
SMEM = functools.partial(pl.BlockSpec, memory_space=pltpu.SMEM)
HBM = functools.partial(pl.BlockSpec, memory_space=pltpu.HBM)


def call(body, in_specs, out_shapes, scratch=(), flops=0, nbytes=0):
    return pl.pallas_call(
        body,
        in_specs=in_specs,
        out_specs=jax.tree.map(lambda _: VMEM(), out_shapes),
        out_shape=out_shapes,
        scratch_shapes=list(scratch),
        compiler_params=pltpu.CompilerParams(vmem_limit_bytes=VMEM_BYTES),
        cost_estimate=pl.CostEstimate(flops=flops, bytes_accessed=nbytes, transcendentals=0),
    )


def product_dims(transpose):
    return (((1,), (1,)), ((), ())) if transpose else (((1,), (0,)), ((), ()))


def block_column(rows_refs, line, index):
    start = pl.multiple_of(index * BS, BS)
    parts = [ref[:, line, :, pl.ds(start, BS)] for ref in rows_refs]
    return jnp.concatenate(parts, axis=0).reshape(-1, BS)


def stage(first, second, first_coords, second_coords, first_count, second_count):
    slots = first.shape[0]

    def body(c1_ref, c2_ref, n1_ref, n2_ref, w1_hbm, w2_hbm, w1_ref, w2_ref, table_ref, feature_ref, sems):
        copies = [
            pltpu.make_async_copy(w1_hbm, w1_ref, sems.at[0]),
            pltpu.make_async_copy(w2_hbm, w2_ref, sems.at[1]),
        ]
        for copy in copies:
            copy.start()
        lane = lax.broadcasted_iota(jnp.int32, table_ref.shape, 1)
        table = jnp.zeros(table_ref.shape, jnp.int32)
        row = lax.broadcasted_iota(jnp.int32, feature_ref.shape, 0)
        place = lax.broadcasted_iota(jnp.int32, feature_ref.shape, 1)
        feature = jnp.zeros(feature_ref.shape, jnp.int32)
        for s in range(slots):
            i = jnp.where(s < n1_ref[0, 0], c1_ref[1, s], HIDDEN)
            j = jnp.where(s < n2_ref[0, 0], c2_ref[0, s], HIDDEN)
            table = jnp.where(lane == s, i, jnp.where(lane == 64 + s, j, table))
            feature = jnp.where(place == s, jnp.where(row == 0, c1_ref[0, s], c2_ref[1, s]), feature)
        table_ref[...] = table.astype(jnp.float32).astype(jnp.bfloat16)
        feature_ref[...] = feature
        for copy in copies:
            copy.wait()

    return call(
        body,
        [SMEM()] * 4 + [HBM()] * 2,
        (
            jax.ShapeDtypeStruct(first.shape, jnp.bfloat16),
            jax.ShapeDtypeStruct(second.shape, jnp.bfloat16),
            jax.ShapeDtypeStruct((16, BS), jnp.bfloat16),
            jax.ShapeDtypeStruct((8, BS), jnp.int32),
        ),
        scratch=[pltpu.SemaphoreType.DMA((2,))],
        flops=first.size,
        nbytes=8 * first.size,
    )(first_coords, second_coords, first_count, second_count, first, second)


def slot_products(rows, first, second, table, feature):
    share = rows[0].shape[2]
    peers = sum(part.shape[0] for part in rows)
    slots = first.shape[0]

    def body(index_ref, table_ref, w1_ref, w2_ref, *refs):
        rows_refs, out_ref = refs[: len(rows)], refs[len(rows)]
        for p in range(peers):
            out_ref[p, 2 * slots] = table_ref[...]
        for base, line, blocks_ref in ((0, 0, w1_ref), (slots, 1, w2_ref)):
            for s in range(slots):
                left = block_column(rows_refs, line, index_ref[line, s])
                product = lax.dot_general(
                    left, blocks_ref[s], product_dims(line > 0), preferred_element_type=jnp.float32
                )
                out_ref[:, base + s] = product.astype(jnp.bfloat16).reshape(peers, share, BS)

    return call(
        body,
        [SMEM()] + [VMEM()] * (len(rows) + 3),
        jax.ShapeDtypeStruct((peers, 2 * slots + 1, share, BS), jnp.bfloat16),
        flops=4 * slots * peers * share * BS * BS,
        nbytes=8 * slots * peers * share * BS,
    )(feature, table, first, second, *rows)


def hidden_step(parts):
    peers, width = parts.shape[0], parts.shape[3]
    slots = parts.shape[1] // 2
    share = parts.shape[2]
    hidden_blocks = HIDDEN

    def body(parts_ref, out_ref, pre, grad, act_blocks, grad_blocks, table, index, sem):
        row = lax.broadcasted_iota(jnp.int32, (peers, width), 0)
        lines = jnp.zeros((peers, width), jnp.float32)
        for p in range(peers):
            lines = jnp.where(row == p, parts_ref[p, 2 * slots].astype(jnp.float32), lines)
        table[...] = lines.astype(jnp.int32)
        copy = pltpu.make_async_copy(table, index, sem)
        copy.start()
        pre[...] = jnp.zeros_like(pre)
        grad[...] = jnp.zeros_like(grad)
        act_blocks[hidden_blocks:] = jnp.zeros((1, share, width), jnp.bfloat16)
        grad_blocks[hidden_blocks:] = jnp.zeros((1, share, width), jnp.bfloat16)
        copy.wait()

        def add(p, carry):
            for s in range(slots):
                for half in range(2):
                    q = p + half * (peers // 2)
                    i, j = index[q, s], index[q, 64 + s]
                    pre[half, i] = pre[half, i] + parts_ref[q, s].astype(jnp.float32)
                    grad[half, j] = grad[half, j] + parts_ref[q, slots + s].astype(jnp.float32)
            return carry

        lax.fori_loop(0, peers // 2, add, 0)

        def point(h, carry):
            value = pre[0, h] + pre[1, h]
            slope = grad[0, h] + grad[1, h]
            gate = 1.0 / (1.0 + jnp.exp(-value))
            act_blocks[h] = (value * gate).astype(jnp.bfloat16)
            grad_blocks[h] = (slope * gate * (1.0 + value * (1.0 - gate))).astype(jnp.bfloat16)
            return carry

        lax.fori_loop(0, hidden_blocks, point, 0, unroll=8)

        def pick(p, carry):
            for s in range(slots):
                out_ref[p, s] = act_blocks[index[p, 64 + s]]
                out_ref[p, slots + s] = grad_blocks[index[p, s]]
            return carry

        lax.fori_loop(0, peers, pick, 0)

    return call(
        body,
        [VMEM()],
        jax.ShapeDtypeStruct((peers, 2 * slots, share, width), jnp.bfloat16),
        scratch=[
            pltpu.VMEM((2, hidden_blocks + 1, share, width), jnp.float32),
            pltpu.VMEM((2, hidden_blocks + 1, share, width), jnp.float32),
            pltpu.VMEM((hidden_blocks + 1, share, width), jnp.bfloat16),
            pltpu.VMEM((hidden_blocks + 1, share, width), jnp.bfloat16),
            pltpu.VMEM((peers, width), jnp.int32),
            pltpu.SMEM((peers, width), jnp.int32),
            pltpu.SemaphoreType.DMA,
        ],
        flops=4 * parts.size,
        nbytes=6 * parts.size,
    )(parts)


def feature_sums(slots_in, first, second, feature):
    peers, both, share, width = slots_in.shape
    slots = both // 2

    def body(index_ref, in_ref, w1_ref, w2_ref, *refs):
        out_refs, total = refs[:-1], refs[-1]
        for base, line, blocks_ref in ((0, 1, w2_ref), (slots, 0, w1_ref)):
            total[...] = jnp.zeros_like(total)
            for s in range(slots):
                left = in_ref[:, base + s].reshape(peers * share, width)
                product = lax.dot_general(
                    left, blocks_ref[s], product_dims(base > 0), preferred_element_type=jnp.float32
                )
                target = index_ref[line, s]
                total[target] = total[target] + product
            place = FEATURE if base else 0
            for k in range(FEATURE):
                value = total[k].astype(jnp.bfloat16).reshape(peers, share, width)
                at = 0
                for ref, places in zip(out_refs, PLACES):
                    ref[:, place + k] = value[at : at + places]
                    at += places

    return call(
        body,
        [SMEM()] + [VMEM()] * 3,
        tuple(
            jax.ShapeDtypeStruct((places, 2 * FEATURE, share, width), jnp.bfloat16) for places in PLACES
        ),
        scratch=[pltpu.VMEM((FEATURE, peers * share, width), jnp.float32)],
        flops=2 * slots_in.size * BS,
        nbytes=4 * slots_in.size,
    )(feature, slots_in, first, second)


def block_grads(rows, slots_in, feature):
    peers, both, share, width = slots_in.shape
    slots = both // 2
    dims = (((0,), (0,)), ((), ()))

    def body(index_ref, *refs):
        rows_refs, (in_ref, out_ref) = refs[: len(rows)], refs[len(rows) :]
        for s in range(slots):
            left = block_column(rows_refs, 0, index_ref[0, s])
            hidden = in_ref[:, slots + s].reshape(peers * share, width)
            grad = lax.dot_general(left, hidden, dims, preferred_element_type=jnp.float32)
            out_ref[s] = grad.astype(jnp.bfloat16)
        for s in range(slots):
            right = block_column(rows_refs, 1, index_ref[1, s])
            hidden = in_ref[:, s].reshape(peers * share, width)
            grad = lax.dot_general(hidden, right, dims, preferred_element_type=jnp.float32)
            out_ref[slots + s] = grad.astype(jnp.bfloat16)

    return call(
        body,
        [SMEM()] + [VMEM()] * (len(rows) + 1),
        jax.ShapeDtypeStruct((both, BS, BS), jnp.bfloat16),
        flops=2 * slots_in.size * BS,
        nbytes=4 * slots_in.size,
    )(feature, *rows, slots_in)


def near_sums(parts, far_place):
    group, blocks, share, width = parts[0].shape
    half = group // 2

    def body(place_ref, *refs):
        part_refs, (low_ref, high_ref), out_refs = refs[:3], refs[3:5], refs[5:]
        for step in range(group):
            k = lax.rem(place_ref[0] + step, group)
            for b in range(blocks):
                pair = lax.rem(k, half)
                total = jnp.where(k < half, low_ref[pair, b], high_ref[pair, b]).astype(jnp.float32)
                for ref in part_refs:
                    total = total + ref[k, b].astype(jnp.float32)
                out_refs[step][b] = total.astype(jnp.bfloat16)

    return call(
        body,
        [SMEM()] + [VMEM()] * len(parts),
        (jax.ShapeDtypeStruct((blocks, share, width), jnp.bfloat16),) * group,
        flops=4 * parts[0].size,
        nbytes=8 * parts[0].size,
    )(far_place, *parts)


def final_sums(parts, grads, others):
    both, share, width = parts[0].shape
    slots = grads.shape[0] // 2

    def body(*refs):
        part_refs, refs = refs[: len(parts)], refs[len(parts) :]
        grads_ref, others_ref, out_ref, in_ref, w1_ref, w2_ref = refs
        for s in range(2 * slots):
            total = grads_ref[s].astype(jnp.float32) + others_ref[s].astype(jnp.float32)
            target = w1_ref if s < slots else w2_ref
            target[0, 0, s % slots] = total.astype(jnp.bfloat16)
        for k in range(both):
            total = part_refs[0][k].astype(jnp.float32)
            for ref in part_refs[1:]:
                total = total + ref[k].astype(jnp.float32)
            target, place = (out_ref, k) if k < FEATURE else (in_ref, k - FEATURE)
            target[:, place * width : (place + 1) * width] = total.astype(jnp.bfloat16)

    row = jax.ShapeDtypeStruct((share, FEATURE * width), jnp.bfloat16)
    grad = jax.ShapeDtypeStruct((1, 1, slots, BS, BS), jnp.bfloat16)
    return call(
        body,
        [VMEM()] * (len(parts) + 2),
        (row, row, grad, grad),
        flops=grads.size,
        nbytes=6 * grads.size,
    )(*parts, grads, others)


def swap(parts, axis):
    return lax.all_to_all(parts, axis, split_axis=0, concat_axis=0, tiled=True)


def send_on(value, hops):
    peers = lax.axis_size("col")
    return lax.ppermute(value, "col", [(c, (c + hops) % peers) for c in range(peers)])


def on_device(tokens, w1_blocks, w1_coords, w1_count, w2_blocks, w2_coords, w2_count, cotangent):
    peers = lax.axis_size("col")
    far = [[c + NEAR * k for k in range(peers // NEAR)] for c in range(NEAR)]

    own = lax.all_gather(jnp.stack([tokens, cotangent]), "col", axis_index_groups=far)
    own, first, second = lax.optimization_barrier((own, w1_blocks, w2_blocks))
    half = len(far[0]) // 2
    rows = [own] + [
        send_on(part, -step)
        for part, step in zip((own, own, own[:half], own[half:]), STEPS[1:])
    ]
    first, second, table, feature = stage(
        first[0, 0], second[0, 0], w1_coords[0, 0].T, w2_coords[0, 0].T, w1_count, w2_count
    )
    parts = swap(slot_products(rows, first, second, table, feature), "row")
    slots_in = swap(hidden_step(parts), "row")
    sums = feature_sums(slots_in, first, second, feature)
    sums = [sums[0]] + [send_on(part, step) for part, step in zip(sums[1:], STEPS[1:])]
    grads = block_grads(rows, slots_in, feature)
    others = lax.ppermute(grads, "tok", [(0, 1), (1, 0)])
    sums = near_sums(sums, lax.div(lax.axis_index("col"), NEAR).reshape(1))
    sums = [sums[0]] + [send_on(sums[k], NEAR * k) for k in range(1, peers // NEAR)]
    return final_sums(sums, grads, others)


def solution(mesh):
    placed = (
        P(("tok", "col"), "row"),
        P("row", "col", None, None, None),
        P("row", "col", None, None),
        P("row", "col"),
        P("row", "col", None, None, None),
        P("row", "col", None, None),
        P("row", "col"),
        P(("tok", "col"), "row"),
    )
    return jax.shard_map(
        on_device,
        mesh=mesh,
        in_specs=placed,
        out_specs=(
            P(("tok", "col"), "row"),
            P(("tok", "col"), "row"),
            P("row", "col", None, None, None),
            P("row", "col", None, None, None),
        ),
        check_vma=False,
    )
```

```python
import functools

import jax
import jax.numpy as jnp
from jax import lax
from jax.experimental import pallas as pl
from jax.experimental.pallas import tpu as pltpu
from jax.sharding import PartitionSpec as P

BS = 128
FEATURE = 8
HIDDEN = 32
NEAR = 4
STEPS = (0, 1, -1, 2, -2)
PLACES = (4, 4, 4, 2, 2)
VMEM_BYTES = 12 * 1024 * 1024

VMEM = functools.partial(pl.BlockSpec, memory_space=pltpu.VMEM)
SMEM = functools.partial(pl.BlockSpec, memory_space=pltpu.SMEM)
HBM = functools.partial(pl.BlockSpec, memory_space=pltpu.HBM)


def call(body, in_specs, out_shapes, scratch=(), flops=0, nbytes=0):
    return pl.pallas_call(
        body,
        in_specs=in_specs,
        out_specs=jax.tree.map(lambda _: VMEM(), out_shapes),
        out_shape=out_shapes,
        scratch_shapes=list(scratch),
        compiler_params=pltpu.CompilerParams(vmem_limit_bytes=VMEM_BYTES),
        cost_estimate=pl.CostEstimate(flops=flops, bytes_accessed=nbytes, transcendentals=0),
    )


def product_dims(transpose):
    return (((1,), (1,)), ((), ())) if transpose else (((1,), (0,)), ((), ()))


def block_column(rows_refs, line, index):
    start = pl.multiple_of(index * BS, BS)
    parts = [ref[:, line, :, pl.ds(start, BS)] for ref in rows_refs]
    return jnp.concatenate(parts, axis=0).reshape(-1, BS)


def stage(first, second, first_coords, second_coords, first_count, second_count):
    slots = first.shape[0]

    def body(c1_ref, c2_ref, n1_ref, n2_ref, w1_hbm, w2_hbm, w1_ref, w2_ref, table_ref, feature_ref, sems):
        copies = [
            pltpu.make_async_copy(w1_hbm, w1_ref, sems.at[0]),
            pltpu.make_async_copy(w2_hbm, w2_ref, sems.at[1]),
        ]
        for copy in copies:
            copy.start()
        lane = lax.broadcasted_iota(jnp.int32, table_ref.shape, 1)
        table = jnp.zeros(table_ref.shape, jnp.int32)
        row = lax.broadcasted_iota(jnp.int32, feature_ref.shape, 0)
        place = lax.broadcasted_iota(jnp.int32, feature_ref.shape, 1)
        feature = jnp.zeros(feature_ref.shape, jnp.int32)
        for s in range(slots):
            i = jnp.where(s < n1_ref[0, 0], c1_ref[1, s], HIDDEN)
            j = jnp.where(s < n2_ref[0, 0], c2_ref[0, s], HIDDEN)
            table = jnp.where(lane == s, i, jnp.where(lane == 64 + s, j, table))
            feature = jnp.where(place == s, jnp.where(row == 0, c1_ref[0, s], c2_ref[1, s]), feature)
        table_ref[...] = table.astype(jnp.float32).astype(jnp.bfloat16)
        feature_ref[...] = feature
        for copy in copies:
            copy.wait()

    return call(
        body,
        [SMEM()] * 4 + [HBM()] * 2,
        (
            jax.ShapeDtypeStruct(first.shape, jnp.bfloat16),
            jax.ShapeDtypeStruct(second.shape, jnp.bfloat16),
            jax.ShapeDtypeStruct((16, BS), jnp.bfloat16),
            jax.ShapeDtypeStruct((8, BS), jnp.int32),
        ),
        scratch=[pltpu.SemaphoreType.DMA((2,))],
        flops=first.size,
        nbytes=8 * first.size,
    )(first_coords, second_coords, first_count, second_count, first, second)


def slot_products(rows, first, second, table, feature):
    share = rows[0].shape[2]
    peers = sum(part.shape[0] for part in rows)
    slots = first.shape[0]

    def body(index_ref, table_ref, w1_ref, w2_ref, *refs):
        rows_refs, out_ref = refs[: len(rows)], refs[len(rows)]
        for p in range(peers):
            out_ref[p, 2 * slots] = table_ref[...]
        for base, line, blocks_ref in ((0, 0, w1_ref), (slots, 1, w2_ref)):
            for s in range(slots):
                left = block_column(rows_refs, line, index_ref[line, s])
                product = lax.dot_general(
                    left, blocks_ref[s], product_dims(line > 0), preferred_element_type=jnp.float32
                )
                out_ref[:, base + s] = product.astype(jnp.bfloat16).reshape(peers, share, BS)

    return call(
        body,
        [SMEM()] + [VMEM()] * (len(rows) + 3),
        jax.ShapeDtypeStruct((peers, 2 * slots + 1, share, BS), jnp.bfloat16),
        flops=4 * slots * peers * share * BS * BS,
        nbytes=8 * slots * peers * share * BS,
    )(feature, table, first, second, *rows)


def hidden_step(parts):
    peers, width = parts.shape[0], parts.shape[3]
    slots = parts.shape[1] // 2
    share = parts.shape[2]
    hidden_blocks = HIDDEN

    def body(parts_ref, out_ref, pre, grad, act_blocks, grad_blocks, table, index, sem):
        row = lax.broadcasted_iota(jnp.int32, (peers, width), 0)
        lines = jnp.zeros((peers, width), jnp.float32)
        for p in range(peers):
            lines = jnp.where(row == p, parts_ref[p, 2 * slots].astype(jnp.float32), lines)
        table[...] = lines.astype(jnp.int32)
        copy = pltpu.make_async_copy(table, index, sem)
        copy.start()
        pre[...] = jnp.zeros_like(pre)
        grad[...] = jnp.zeros_like(grad)
        act_blocks[hidden_blocks:] = jnp.zeros((1, share, width), jnp.bfloat16)
        grad_blocks[hidden_blocks:] = jnp.zeros((1, share, width), jnp.bfloat16)
        copy.wait()

        def add(p, carry):
            for s in range(slots):
                for half in range(2):
                    q = p + half * (peers // 2)
                    i, j = index[q, s], index[q, 64 + s]
                    pre[half, i] = pre[half, i] + parts_ref[q, s].astype(jnp.float32)
                    grad[half, j] = grad[half, j] + parts_ref[q, slots + s].astype(jnp.float32)
            return carry

        lax.fori_loop(0, peers // 2, add, 0)

        def point(h, carry):
            value = pre[0, h] + pre[1, h]
            slope = grad[0, h] + grad[1, h]
            gate = 1.0 / (1.0 + jnp.exp(-value))
            act_blocks[h] = (value * gate).astype(jnp.bfloat16)
            grad_blocks[h] = (slope * gate * (1.0 + value * (1.0 - gate))).astype(jnp.bfloat16)
            return carry

        lax.fori_loop(0, hidden_blocks, point, 0, unroll=8)

        def pick(p, carry):
            for s in range(slots):
                out_ref[p, s] = act_blocks[index[p, 64 + s]]
                out_ref[p, slots + s] = grad_blocks[index[p, s]]
            return carry

        lax.fori_loop(0, peers, pick, 0)

    return call(
        body,
        [VMEM()],
        jax.ShapeDtypeStruct((peers, 2 * slots, share, width), jnp.bfloat16),
        scratch=[
            pltpu.VMEM((2, hidden_blocks + 1, share, width), jnp.float32),
            pltpu.VMEM((2, hidden_blocks + 1, share, width), jnp.float32),
            pltpu.VMEM((hidden_blocks + 1, share, width), jnp.bfloat16),
            pltpu.VMEM((hidden_blocks + 1, share, width), jnp.bfloat16),
            pltpu.VMEM((peers, width), jnp.int32),
            pltpu.SMEM((peers, width), jnp.int32),
            pltpu.SemaphoreType.DMA,
        ],
        flops=4 * parts.size,
        nbytes=6 * parts.size,
    )(parts)


def feature_sums(slots_in, first, second, feature):
    peers, both, share, width = slots_in.shape
    slots = both // 2

    def body(index_ref, in_ref, w1_ref, w2_ref, *refs):
        out_refs, total = refs[:-1], refs[-1]
        for base, line, blocks_ref in ((0, 1, w2_ref), (slots, 0, w1_ref)):
            total[...] = jnp.zeros_like(total)
            for s in range(slots):
                left = in_ref[:, base + s].reshape(peers * share, width)
                product = lax.dot_general(
                    left, blocks_ref[s], product_dims(base > 0), preferred_element_type=jnp.float32
                )
                target = index_ref[line, s]
                total[target] = total[target] + product
            place = FEATURE if base else 0
            for k in range(FEATURE):
                value = total[k].astype(jnp.bfloat16).reshape(peers, share, width)
                at = 0
                for ref, places in zip(out_refs, PLACES):
                    ref[:, place + k] = value[at : at + places]
                    at += places

    return call(
        body,
        [SMEM()] + [VMEM()] * 3,
        tuple(
            jax.ShapeDtypeStruct((places, 2 * FEATURE, share, width), jnp.bfloat16) for places in PLACES
        ),
        scratch=[pltpu.VMEM((FEATURE, peers * share, width), jnp.float32)],
        flops=2 * slots_in.size * BS,
        nbytes=4 * slots_in.size,
    )(feature, slots_in, first, second)


def block_grads(rows, slots_in, feature):
    peers, both, share, width = slots_in.shape
    slots = both // 2
    dims = (((0,), (0,)), ((), ()))

    def body(index_ref, *refs):
        rows_refs, (in_ref, out_ref) = refs[: len(rows)], refs[len(rows) :]
        for s in range(slots):
            left = block_column(rows_refs, 0, index_ref[0, s])
            hidden = in_ref[:, slots + s].reshape(peers * share, width)
            grad = lax.dot_general(left, hidden, dims, preferred_element_type=jnp.float32)
            out_ref[s] = grad.astype(jnp.bfloat16)
        for s in range(slots):
            right = block_column(rows_refs, 1, index_ref[1, s])
            hidden = in_ref[:, s].reshape(peers * share, width)
            grad = lax.dot_general(hidden, right, dims, preferred_element_type=jnp.float32)
            out_ref[slots + s] = grad.astype(jnp.bfloat16)

    return call(
        body,
        [SMEM()] + [VMEM()] * (len(rows) + 1),
        jax.ShapeDtypeStruct((both, BS, BS), jnp.bfloat16),
        flops=2 * slots_in.size * BS,
        nbytes=4 * slots_in.size,
    )(feature, *rows, slots_in)


def near_sums(parts):
    group, blocks, share, width = parts[0].shape
    half = group // 2

    def body(*refs):
        part_refs, halves, out_ref = refs[:3], refs[3:5], refs[5]
        for k in range(group):
            for b in range(blocks):
                total = halves[k // half][k % half, b].astype(jnp.float32)
                for ref in part_refs:
                    total = total + ref[k, b].astype(jnp.float32)
                out_ref[k, b] = total.astype(jnp.bfloat16)

    return call(
        body,
        [VMEM()] * len(parts),
        jax.ShapeDtypeStruct((group, blocks, share, width), jnp.bfloat16),
        flops=4 * parts[0].size,
        nbytes=8 * parts[0].size,
    )(*parts)


def final_sums(parts, grads, others):
    group, both, share, width = parts.shape
    slots = grads.shape[0] // 2

    def body(parts_ref, grads_ref, others_ref, out_ref, in_ref, w1_ref, w2_ref):
        for s in range(2 * slots):
            total = grads_ref[s].astype(jnp.float32) + others_ref[s].astype(jnp.float32)
            target = w1_ref if s < slots else w2_ref
            target[0, 0, s % slots] = total.astype(jnp.bfloat16)
        for k in range(both):
            total = parts_ref[0, k].astype(jnp.float32)
            for c in range(1, group):
                total = total + parts_ref[c, k].astype(jnp.float32)
            target, place = (out_ref, k) if k < FEATURE else (in_ref, k - FEATURE)
            target[:, place * width : (place + 1) * width] = total.astype(jnp.bfloat16)

    row = jax.ShapeDtypeStruct((share, FEATURE * width), jnp.bfloat16)
    grad = jax.ShapeDtypeStruct((1, 1, slots, BS, BS), jnp.bfloat16)
    return call(
        body, [VMEM()] * 3, (row, row, grad, grad), flops=grads.size, nbytes=6 * grads.size
    )(parts, grads, others)


def swap(parts, axis, groups=None):
    return lax.all_to_all(
        parts, axis, split_axis=0, concat_axis=0, tiled=True, axis_index_groups=groups
    )


def send_on(value, hops):
    peers = lax.axis_size("col")
    return lax.ppermute(value, "col", [(c, (c + hops) % peers) for c in range(peers)])


def on_device(tokens, w1_blocks, w1_coords, w1_count, w2_blocks, w2_coords, w2_count, cotangent):
    peers = lax.axis_size("col")
    far = [[c + NEAR * k for k in range(peers // NEAR)] for c in range(NEAR)]

    own = lax.all_gather(jnp.stack([tokens, cotangent]), "col", axis_index_groups=far)
    own, first, second = lax.optimization_barrier((own, w1_blocks, w2_blocks))
    half = len(far[0]) // 2
    rows = [own] + [
        send_on(part, -step)
        for part, step in zip((own, own, own[:half], own[half:]), STEPS[1:])
    ]
    first, second, table, feature = stage(
        first[0, 0], second[0, 0], w1_coords[0, 0].T, w2_coords[0, 0].T, w1_count, w2_count
    )
    parts = swap(slot_products(rows, first, second, table, feature), "row")
    slots_in = swap(hidden_step(parts), "row")
    sums = feature_sums(slots_in, first, second, feature)
    sums = [sums[0]] + [send_on(part, step) for part, step in zip(sums[1:], STEPS[1:])]
    grads = block_grads(rows, slots_in, feature)
    others = lax.ppermute(grads, "tok", [(0, 1), (1, 0)])
    sums = swap(near_sums(sums), "col", far)
    return final_sums(sums, grads, others)


def solution(mesh):
    placed = (
        P(("tok", "col"), "row"),
        P("row", "col", None, None, None),
        P("row", "col", None, None),
        P("row", "col"),
        P("row", "col", None, None, None),
        P("row", "col", None, None),
        P("row", "col"),
        P(("tok", "col"), "row"),
    )
    return jax.shard_map(
        on_device,
        mesh=mesh,
        in_specs=placed,
        out_specs=(
            P(("tok", "col"), "row"),
            P(("tok", "col"), "row"),
            P("row", "col", None, None, None),
            P("row", "col", None, None, None),
        ),
        check_vma=False,
    )
```

```python
import functools

import jax
import jax.numpy as jnp
from jax import lax
from jax.experimental import pallas as pl
from jax.experimental.pallas import tpu as pltpu
from jax.sharding import PartitionSpec as P

BS = 128
FEATURE = 8
HIDDEN = 32
NEAR = 4
STEPS = (0, 1, -1, 2, -2)
PLACES = (4, 4, 4, 2, 2)
VMEM_BYTES = 12 * 1024 * 1024

VMEM = functools.partial(pl.BlockSpec, memory_space=pltpu.VMEM)
SMEM = functools.partial(pl.BlockSpec, memory_space=pltpu.SMEM)
HBM = functools.partial(pl.BlockSpec, memory_space=pltpu.HBM)


def call(body, in_specs, out_shapes, scratch=(), flops=0, nbytes=0):
    return pl.pallas_call(
        body,
        in_specs=in_specs,
        out_specs=jax.tree.map(lambda _: VMEM(), out_shapes),
        out_shape=out_shapes,
        scratch_shapes=list(scratch),
        compiler_params=pltpu.CompilerParams(vmem_limit_bytes=VMEM_BYTES),
        cost_estimate=pl.CostEstimate(flops=flops, bytes_accessed=nbytes, transcendentals=0),
    )


def product_dims(transpose):
    return (((1,), (1,)), ((), ())) if transpose else (((1,), (0,)), ((), ()))


def block_column(rows_refs, line, index):
    start = pl.multiple_of(index * BS, BS)
    parts = [ref[:, line, :, pl.ds(start, BS)] for ref in rows_refs]
    return jnp.concatenate(parts, axis=0).reshape(-1, BS)


def stage(first, second, first_coords, second_coords, first_count, second_count):
    slots = first.shape[0]

    def body(n1_ref, n2_ref, *refs):
        sources, (w1_ref, w2_ref, table_ref, feature_ref) = refs[:4], refs[4:8]
        c1_ref, c2_ref, sems = refs[8:]
        targets = (c1_ref, c2_ref, w1_ref, w2_ref)
        copies = [
            pltpu.make_async_copy(x, y, sems.at[i]) for i, (x, y) in enumerate(zip(sources, targets))
        ]
        for copy in copies:
            copy.start()
        for copy in copies[:2]:
            copy.wait()
        lane = lax.broadcasted_iota(jnp.int32, table_ref.shape, 1)
        table = jnp.zeros(table_ref.shape, jnp.int32)
        row = lax.broadcasted_iota(jnp.int32, feature_ref.shape, 0)
        place = lax.broadcasted_iota(jnp.int32, feature_ref.shape, 1)
        feature = jnp.zeros(feature_ref.shape, jnp.int32)
        for s in range(slots):
            i = jnp.where(s < n1_ref[0, 0], c1_ref[1, s], HIDDEN)
            j = jnp.where(s < n2_ref[0, 0], c2_ref[0, s], HIDDEN)
            table = jnp.where(lane == s, i, jnp.where(lane == 64 + s, j, table))
            feature = jnp.where(place == s, jnp.where(row == 0, c1_ref[0, s], c2_ref[1, s]), feature)
        table_ref[...] = table.astype(jnp.float32).astype(jnp.bfloat16)
        feature_ref[...] = feature
        for copy in copies[2:]:
            copy.wait()

    return call(
        body,
        [SMEM()] * 2 + [HBM()] * 4,
        (
            jax.ShapeDtypeStruct(first.shape, jnp.bfloat16),
            jax.ShapeDtypeStruct(second.shape, jnp.bfloat16),
            jax.ShapeDtypeStruct((16, BS), jnp.bfloat16),
            jax.ShapeDtypeStruct((8, BS), jnp.int32),
        ),
        scratch=[
            pltpu.SMEM(first_coords.shape, jnp.int32),
            pltpu.SMEM(second_coords.shape, jnp.int32),
            pltpu.SemaphoreType.DMA((4,)),
        ],
        flops=first.size,
        nbytes=8 * first.size,
    )(
        first_count,
        second_count,
        *(
            pltpu.with_memory_space_constraint(value, pltpu.HBM)
            for value in (first_coords, second_coords, first, second)
        ),
    )


def slot_products(rows, first, second, table, feature):
    share = rows[0].shape[2]
    peers = sum(part.shape[0] for part in rows)
    slots = first.shape[0]

    def body(index_ref, table_ref, w1_ref, w2_ref, *refs):
        rows_refs, out_ref = refs[: len(rows)], refs[len(rows)]
        for p in range(peers):
            out_ref[p, 2 * slots] = table_ref[...]
        for base, line, blocks_ref in ((0, 0, w1_ref), (slots, 1, w2_ref)):
            for s in range(slots):
                left = block_column(rows_refs, line, index_ref[line, s])
                product = lax.dot_general(
                    left, blocks_ref[s], product_dims(line > 0), preferred_element_type=jnp.float32
                )
                out_ref[:, base + s] = product.astype(jnp.bfloat16).reshape(peers, share, BS)

    return call(
        body,
        [SMEM()] + [VMEM()] * (len(rows) + 3),
        jax.ShapeDtypeStruct((peers, 2 * slots + 1, share, BS), jnp.bfloat16),
        flops=4 * slots * peers * share * BS * BS,
        nbytes=8 * slots * peers * share * BS,
    )(feature, table, first, second, *rows)


def hidden_step(parts):
    peers, width = parts.shape[0], parts.shape[3]
    slots = parts.shape[1] // 2
    share = parts.shape[2]
    hidden_blocks = HIDDEN

    def body(parts_ref, out_ref, pre, grad, act_blocks, grad_blocks, table, index, sem):
        row = lax.broadcasted_iota(jnp.int32, (peers, width), 0)
        lines = jnp.zeros((peers, width), jnp.float32)
        for p in range(peers):
            lines = jnp.where(row == p, parts_ref[p, 2 * slots].astype(jnp.float32), lines)
        table[...] = lines.astype(jnp.int32)
        copy = pltpu.make_async_copy(table, index, sem)
        copy.start()
        pre[...] = jnp.zeros_like(pre)
        grad[...] = jnp.zeros_like(grad)
        act_blocks[hidden_blocks:] = jnp.zeros((1, share, width), jnp.bfloat16)
        grad_blocks[hidden_blocks:] = jnp.zeros((1, share, width), jnp.bfloat16)
        copy.wait()

        def add(p, carry):
            for s in range(slots):
                for half in range(2):
                    q = p + half * (peers // 2)
                    i, j = index[q, s], index[q, 64 + s]
                    pre[half, i] = pre[half, i] + parts_ref[q, s].astype(jnp.float32)
                    grad[half, j] = grad[half, j] + parts_ref[q, slots + s].astype(jnp.float32)
            return carry

        lax.fori_loop(0, peers // 2, add, 0)

        def point(h, carry):
            value = pre[0, h] + pre[1, h]
            slope = grad[0, h] + grad[1, h]
            gate = 1.0 / (1.0 + jnp.exp(-value))
            act_blocks[h] = (value * gate).astype(jnp.bfloat16)
            grad_blocks[h] = (slope * gate * (1.0 + value * (1.0 - gate))).astype(jnp.bfloat16)
            return carry

        lax.fori_loop(0, hidden_blocks, point, 0, unroll=8)

        def pick(p, carry):
            for s in range(slots):
                out_ref[p, s] = act_blocks[index[p, 64 + s]]
                out_ref[p, slots + s] = grad_blocks[index[p, s]]
            return carry

        lax.fori_loop(0, peers, pick, 0)

    return call(
        body,
        [VMEM()],
        jax.ShapeDtypeStruct((peers, 2 * slots, share, width), jnp.bfloat16),
        scratch=[
            pltpu.VMEM((2, hidden_blocks + 1, share, width), jnp.float32),
            pltpu.VMEM((2, hidden_blocks + 1, share, width), jnp.float32),
            pltpu.VMEM((hidden_blocks + 1, share, width), jnp.bfloat16),
            pltpu.VMEM((hidden_blocks + 1, share, width), jnp.bfloat16),
            pltpu.VMEM((peers, width), jnp.int32),
            pltpu.SMEM((peers, width), jnp.int32),
            pltpu.SemaphoreType.DMA,
        ],
        flops=4 * parts.size,
        nbytes=6 * parts.size,
    )(parts)


def feature_sums(slots_in, first, second, feature):
    peers, both, share, width = slots_in.shape
    slots = both // 2

    def body(index_ref, in_ref, w1_ref, w2_ref, *refs):
        out_refs, total = refs[:-1], refs[-1]
        for base, line, blocks_ref in ((0, 1, w2_ref), (slots, 0, w1_ref)):
            total[...] = jnp.zeros_like(total)
            for s in range(slots):
                left = in_ref[:, base + s].reshape(peers * share, width)
                product = lax.dot_general(
                    left, blocks_ref[s], product_dims(base > 0), preferred_element_type=jnp.float32
                )
                target = index_ref[line, s]
                total[target] = total[target] + product
            place = FEATURE if base else 0
            for k in range(FEATURE):
                value = total[k].astype(jnp.bfloat16).reshape(peers, share, width)
                at = 0
                for ref, places in zip(out_refs, PLACES):
                    ref[:, place + k] = value[at : at + places]
                    at += places

    return call(
        body,
        [SMEM()] + [VMEM()] * 3,
        tuple(
            jax.ShapeDtypeStruct((places, 2 * FEATURE, share, width), jnp.bfloat16) for places in PLACES
        ),
        scratch=[pltpu.VMEM((FEATURE, peers * share, width), jnp.float32)],
        flops=2 * slots_in.size * BS,
        nbytes=4 * slots_in.size,
    )(feature, slots_in, first, second)


def block_grads(rows, slots_in, feature):
    peers, both, share, width = slots_in.shape
    slots = both // 2
    dims = (((0,), (0,)), ((), ()))

    def body(index_ref, *refs):
        rows_refs, (in_ref, out_ref) = refs[: len(rows)], refs[len(rows) :]
        for s in range(slots):
            left = block_column(rows_refs, 0, index_ref[0, s])
            hidden = in_ref[:, slots + s].reshape(peers * share, width)
            grad = lax.dot_general(left, hidden, dims, preferred_element_type=jnp.float32)
            out_ref[s] = grad.astype(jnp.bfloat16)
        for s in range(slots):
            right = block_column(rows_refs, 1, index_ref[1, s])
            hidden = in_ref[:, s].reshape(peers * share, width)
            grad = lax.dot_general(hidden, right, dims, preferred_element_type=jnp.float32)
            out_ref[slots + s] = grad.astype(jnp.bfloat16)

    return call(
        body,
        [SMEM()] + [VMEM()] * (len(rows) + 1),
        jax.ShapeDtypeStruct((both, BS, BS), jnp.bfloat16),
        flops=2 * slots_in.size * BS,
        nbytes=4 * slots_in.size,
    )(feature, *rows, slots_in)


def near_sums(parts):
    group, blocks, share, width = parts[0].shape
    half = group // 2

    def body(*refs):
        part_refs, halves, out_ref = refs[:3], refs[3:5], refs[5]
        for k in range(group):
            for b in range(blocks):
                total = halves[k // half][k % half, b].astype(jnp.float32)
                for ref in part_refs:
                    total = total + ref[k, b].astype(jnp.float32)
                out_ref[k, b] = total.astype(jnp.bfloat16)

    return call(
        body,
        [VMEM()] * len(parts),
        jax.ShapeDtypeStruct((group, blocks, share, width), jnp.bfloat16),
        flops=4 * parts[0].size,
        nbytes=8 * parts[0].size,
    )(*parts)


def final_sums(parts, grads, others):
    group, both, share, width = parts.shape
    slots = grads.shape[0] // 2

    def body(parts_ref, grads_ref, others_ref, out_ref, in_ref, w1_ref, w2_ref):
        for s in range(2 * slots):
            total = grads_ref[s].astype(jnp.float32) + others_ref[s].astype(jnp.float32)
            target = w1_ref if s < slots else w2_ref
            target[0, 0, s % slots] = total.astype(jnp.bfloat16)
        for k in range(both):
            total = parts_ref[0, k].astype(jnp.float32)
            for c in range(1, group):
                total = total + parts_ref[c, k].astype(jnp.float32)
            target, place = (out_ref, k) if k < FEATURE else (in_ref, k - FEATURE)
            target[:, place * width : (place + 1) * width] = total.astype(jnp.bfloat16)

    row = jax.ShapeDtypeStruct((share, FEATURE * width), jnp.bfloat16)
    grad = jax.ShapeDtypeStruct((1, 1, slots, BS, BS), jnp.bfloat16)
    return call(
        body, [VMEM()] * 3, (row, row, grad, grad), flops=grads.size, nbytes=6 * grads.size
    )(parts, grads, others)


def swap(parts, axis, groups=None):
    return lax.all_to_all(
        parts, axis, split_axis=0, concat_axis=0, tiled=True, axis_index_groups=groups
    )


def send_on(value, hops):
    peers = lax.axis_size("col")
    return lax.ppermute(value, "col", [(c, (c + hops) % peers) for c in range(peers)])


def on_device(tokens, w1_blocks, w1_coords, w1_count, w2_blocks, w2_coords, w2_count, cotangent):
    peers = lax.axis_size("col")
    far = [[c + NEAR * k for k in range(peers // NEAR)] for c in range(NEAR)]

    own = lax.all_gather(jnp.stack([tokens, cotangent]), "col", axis_index_groups=far)
    own, first, second = lax.optimization_barrier((own, w1_blocks, w2_blocks))
    half = len(far[0]) // 2
    rows = [own] + [
        send_on(part, -step)
        for part, step in zip((own, own, own[:half], own[half:]), STEPS[1:])
    ]
    first, second, table, feature = stage(
        first[0, 0], second[0, 0], w1_coords[0, 0].T, w2_coords[0, 0].T, w1_count, w2_count
    )
    parts = swap(slot_products(rows, first, second, table, feature), "row")
    slots_in = swap(hidden_step(parts), "row")
    sums = feature_sums(slots_in, first, second, feature)
    sums = [sums[0]] + [send_on(part, step) for part, step in zip(sums[1:], STEPS[1:])]
    grads = block_grads(rows, slots_in, feature)
    others = lax.ppermute(grads, "tok", [(0, 1), (1, 0)])
    sums = swap(near_sums(sums), "col", far)
    return final_sums(sums, grads, others)


def solution(mesh):
    placed = (
        P(("tok", "col"), "row"),
        P("row", "col", None, None, None),
        P("row", "col", None, None),
        P("row", "col"),
        P("row", "col", None, None, None),
        P("row", "col", None, None),
        P("row", "col"),
        P(("tok", "col"), "row"),
    )
    return jax.shard_map(
        on_device,
        mesh=mesh,
        in_specs=placed,
        out_specs=(
            P(("tok", "col"), "row"),
            P(("tok", "col"), "row"),
            P("row", "col", None, None, None),
            P("row", "col", None, None, None),
        ),
        check_vma=False,
    )
```

```python
import functools

import jax
import jax.numpy as jnp
from jax import lax
from jax.experimental import pallas as pl
from jax.experimental.pallas import tpu as pltpu
from jax.sharding import PartitionSpec as P

BS = 128
FEATURE = 8
HIDDEN = 32
NEAR = 4
TOTALS = 4
STEPS = (0, 1, -1, 2, -2)
PLACES = (4, 4, 4, 2, 2)
VMEM_BYTES = 12 * 1024 * 1024

VMEM = functools.partial(pl.BlockSpec, memory_space=pltpu.VMEM)
SMEM = functools.partial(pl.BlockSpec, memory_space=pltpu.SMEM)
HBM = functools.partial(pl.BlockSpec, memory_space=pltpu.HBM)


def call(body, in_specs, out_shapes, scratch=(), flops=0, nbytes=0):
    return pl.pallas_call(
        body,
        in_specs=in_specs,
        out_specs=jax.tree.map(lambda _: VMEM(), out_shapes),
        out_shape=out_shapes,
        scratch_shapes=list(scratch),
        compiler_params=pltpu.CompilerParams(vmem_limit_bytes=VMEM_BYTES),
        cost_estimate=pl.CostEstimate(flops=flops, bytes_accessed=nbytes, transcendentals=0),
    )


def product_dims(transpose):
    return (((1,), (1,)), ((), ())) if transpose else (((1,), (0,)), ((), ()))


def block_column(rows_refs, line, index):
    start = pl.multiple_of(index * BS, BS)
    parts = [ref[:, line, :, pl.ds(start, BS)] for ref in rows_refs]
    return jnp.concatenate(parts, axis=0).reshape(-1, BS)


def stage(first, second, first_coords, second_coords, first_count, second_count):
    slots = first.shape[0]

    def body(n1_ref, n2_ref, *refs):
        sources, (w1_ref, w2_ref, table_ref, feature_ref) = refs[:4], refs[4:8]
        c1_ref, c2_ref, sems = refs[8:]
        targets = (c1_ref, c2_ref, w1_ref, w2_ref)
        copies = [
            pltpu.make_async_copy(x, y, sems.at[i]) for i, (x, y) in enumerate(zip(sources, targets))
        ]
        for copy in copies:
            copy.start()
        for copy in copies[:2]:
            copy.wait()
        lane = lax.broadcasted_iota(jnp.int32, table_ref.shape, 1)
        table = jnp.zeros(table_ref.shape, jnp.int32)
        row = lax.broadcasted_iota(jnp.int32, feature_ref.shape, 0)
        place = lax.broadcasted_iota(jnp.int32, feature_ref.shape, 1)
        feature = jnp.zeros(feature_ref.shape, jnp.int32)
        for s in range(slots):
            i = jnp.where(s < n1_ref[0, 0], c1_ref[1, s], HIDDEN)
            j = jnp.where(s < n2_ref[0, 0], c2_ref[0, s], HIDDEN)
            table = jnp.where(lane == s, i, jnp.where(lane == 64 + s, j, table))
            feature = jnp.where(place == s, jnp.where(row == 0, c1_ref[0, s], c2_ref[1, s]), feature)
        table_ref[...] = table.astype(jnp.float32).astype(jnp.bfloat16)
        feature_ref[...] = feature
        for copy in copies[2:]:
            copy.wait()

    return call(
        body,
        [SMEM()] * 2 + [HBM()] * 4,
        (
            jax.ShapeDtypeStruct(first.shape, jnp.bfloat16),
            jax.ShapeDtypeStruct(second.shape, jnp.bfloat16),
            jax.ShapeDtypeStruct((16, BS), jnp.bfloat16),
            jax.ShapeDtypeStruct((8, BS), jnp.int32),
        ),
        scratch=[
            pltpu.SMEM(first_coords.shape, jnp.int32),
            pltpu.SMEM(second_coords.shape, jnp.int32),
            pltpu.SemaphoreType.DMA((4,)),
        ],
        flops=first.size,
        nbytes=8 * first.size,
    )(
        first_count,
        second_count,
        *(
            pltpu.with_memory_space_constraint(value, pltpu.HBM)
            for value in (first_coords, second_coords, first, second)
        ),
    )


def slot_products(rows, first, second, table, feature):
    share = rows[0].shape[2]
    peers = sum(part.shape[0] for part in rows)
    slots = first.shape[0]

    def body(index_ref, table_ref, w1_ref, w2_ref, *refs):
        rows_refs, out_ref = refs[: len(rows)], refs[len(rows)]
        for p in range(peers):
            out_ref[p, 2 * slots] = table_ref[...]
        for base, line, blocks_ref in ((0, 0, w1_ref), (slots, 1, w2_ref)):
            for s in range(slots):
                left = block_column(rows_refs, line, index_ref[line, s])
                product = lax.dot_general(
                    left, blocks_ref[s], product_dims(line > 0), preferred_element_type=jnp.float32
                )
                out_ref[:, base + s] = product.astype(jnp.bfloat16).reshape(peers, share, BS)

    return call(
        body,
        [SMEM()] + [VMEM()] * (len(rows) + 3),
        jax.ShapeDtypeStruct((peers, 2 * slots + 1, share, BS), jnp.bfloat16),
        flops=4 * slots * peers * share * BS * BS,
        nbytes=8 * slots * peers * share * BS,
    )(feature, table, first, second, *rows)


def hidden_step(parts):
    peers, width = parts.shape[0], parts.shape[3]
    slots = parts.shape[1] // 2
    share = parts.shape[2]
    hidden_blocks = HIDDEN

    def body(parts_ref, out_ref, *refs):
        pre, grad = refs[:TOTALS], refs[TOTALS : 2 * TOTALS]
        act_blocks, grad_blocks, table, index, sem = refs[2 * TOTALS :]
        row = lax.broadcasted_iota(jnp.int32, (peers, width), 0)
        lines = jnp.zeros((peers, width), jnp.float32)
        for p in range(peers):
            lines = jnp.where(row == p, parts_ref[p, 2 * slots].astype(jnp.float32), lines)
        table[...] = lines.astype(jnp.int32)
        copy = pltpu.make_async_copy(table, index, sem)
        copy.start()
        for total in pre + grad:
            total[...] = jnp.zeros_like(total)
        act_blocks[hidden_blocks:] = jnp.zeros((1, share, width), jnp.bfloat16)
        grad_blocks[hidden_blocks:] = jnp.zeros((1, share, width), jnp.bfloat16)
        copy.wait()

        def add(p, carry):
            for s in range(slots):
                for t in range(TOTALS):
                    q = p + t * (peers // TOTALS)
                    i, j = index[q, s], index[q, 64 + s]
                    pre[t][i] = pre[t][i] + parts_ref[q, s].astype(jnp.float32)
                    grad[t][j] = grad[t][j] + parts_ref[q, slots + s].astype(jnp.float32)
            return carry

        lax.fori_loop(0, peers // TOTALS, add, 0)

        def point(h, carry):
            value = sum(total[h] for total in pre[1:]) + pre[0][h]
            slope = sum(total[h] for total in grad[1:]) + grad[0][h]
            gate = 1.0 / (1.0 + jnp.exp(-value))
            act_blocks[h] = (value * gate).astype(jnp.bfloat16)
            grad_blocks[h] = (slope * gate * (1.0 + value * (1.0 - gate))).astype(jnp.bfloat16)
            return carry

        lax.fori_loop(0, hidden_blocks, point, 0, unroll=8)

        def pick(p, carry):
            for s in range(slots):
                out_ref[p, s] = act_blocks[index[p, 64 + s]]
                out_ref[p, slots + s] = grad_blocks[index[p, s]]
            return carry

        lax.fori_loop(0, peers, pick, 0)

    return call(
        body,
        [VMEM()],
        jax.ShapeDtypeStruct((peers, 2 * slots, share, width), jnp.bfloat16),
        scratch=[
            *[pltpu.VMEM((hidden_blocks + 1, share, width), jnp.float32)] * (2 * TOTALS),
            pltpu.VMEM((hidden_blocks + 1, share, width), jnp.bfloat16),
            pltpu.VMEM((hidden_blocks + 1, share, width), jnp.bfloat16),
            pltpu.VMEM((peers, width), jnp.int32),
            pltpu.SMEM((peers, width), jnp.int32),
            pltpu.SemaphoreType.DMA,
        ],
        flops=4 * parts.size,
        nbytes=6 * parts.size,
    )(parts)


def feature_sums(slots_in, first, second, feature):
    peers, both, share, width = slots_in.shape
    slots = both // 2

    def body(index_ref, in_ref, w1_ref, w2_ref, *refs):
        out_refs, total = refs[:-1], refs[-1]
        for base, line, blocks_ref in ((0, 1, w2_ref), (slots, 0, w1_ref)):
            total[...] = jnp.zeros_like(total)
            for s in range(slots):
                left = in_ref[:, base + s].reshape(peers * share, width)
                product = lax.dot_general(
                    left, blocks_ref[s], product_dims(base > 0), preferred_element_type=jnp.float32
                )
                target = index_ref[line, s]
                total[target] = total[target] + product
            place = FEATURE if base else 0
            for k in range(FEATURE):
                value = total[k].astype(jnp.bfloat16).reshape(peers, share, width)
                at = 0
                for ref, places in zip(out_refs, PLACES):
                    ref[:, place + k] = value[at : at + places]
                    at += places

    return call(
        body,
        [SMEM()] + [VMEM()] * 3,
        tuple(
            jax.ShapeDtypeStruct((places, 2 * FEATURE, share, width), jnp.bfloat16) for places in PLACES
        ),
        scratch=[pltpu.VMEM((FEATURE, peers * share, width), jnp.float32)],
        flops=2 * slots_in.size * BS,
        nbytes=4 * slots_in.size,
    )(feature, slots_in, first, second)


def block_grads(rows, slots_in, feature):
    peers, both, share, width = slots_in.shape
    slots = both // 2
    dims = (((0,), (0,)), ((), ()))

    def body(index_ref, *refs):
        rows_refs, (in_ref, out_ref) = refs[: len(rows)], refs[len(rows) :]
        for s in range(slots):
            left = block_column(rows_refs, 0, index_ref[0, s])
            hidden = in_ref[:, slots + s].reshape(peers * share, width)
            grad = lax.dot_general(left, hidden, dims, preferred_element_type=jnp.float32)
            out_ref[s] = grad.astype(jnp.bfloat16)
        for s in range(slots):
            right = block_column(rows_refs, 1, index_ref[1, s])
            hidden = in_ref[:, s].reshape(peers * share, width)
            grad = lax.dot_general(hidden, right, dims, preferred_element_type=jnp.float32)
            out_ref[slots + s] = grad.astype(jnp.bfloat16)

    return call(
        body,
        [SMEM()] + [VMEM()] * (len(rows) + 1),
        jax.ShapeDtypeStruct((both, BS, BS), jnp.bfloat16),
        flops=2 * slots_in.size * BS,
        nbytes=4 * slots_in.size,
    )(feature, *rows, slots_in)


def near_sums(parts):
    group, blocks, share, width = parts[0].shape
    half = group // 2

    def body(*refs):
        part_refs, halves, out_ref = refs[:3], refs[3:5], refs[5]
        for k in range(group):
            for b in range(blocks):
                total = halves[k // half][k % half, b].astype(jnp.float32)
                for ref in part_refs:
                    total = total + ref[k, b].astype(jnp.float32)
                out_ref[k, b] = total.astype(jnp.bfloat16)

    return call(
        body,
        [VMEM()] * len(parts),
        jax.ShapeDtypeStruct((group, blocks, share, width), jnp.bfloat16),
        flops=4 * parts[0].size,
        nbytes=8 * parts[0].size,
    )(*parts)


def final_sums(parts, grads, others):
    group, both, share, width = parts.shape
    slots = grads.shape[0] // 2

    def body(parts_ref, grads_ref, others_ref, out_ref, in_ref, w1_ref, w2_ref):
        for s in range(2 * slots):
            total = grads_ref[s].astype(jnp.float32) + others_ref[s].astype(jnp.float32)
            target = w1_ref if s < slots else w2_ref
            target[0, 0, s % slots] = total.astype(jnp.bfloat16)
        for k in range(both):
            total = parts_ref[0, k].astype(jnp.float32)
            for c in range(1, group):
                total = total + parts_ref[c, k].astype(jnp.float32)
            target, place = (out_ref, k) if k < FEATURE else (in_ref, k - FEATURE)
            target[:, place * width : (place + 1) * width] = total.astype(jnp.bfloat16)

    row = jax.ShapeDtypeStruct((share, FEATURE * width), jnp.bfloat16)
    grad = jax.ShapeDtypeStruct((1, 1, slots, BS, BS), jnp.bfloat16)
    return call(
        body, [VMEM()] * 3, (row, row, grad, grad), flops=grads.size, nbytes=6 * grads.size
    )(parts, grads, others)


def swap(parts, axis, groups=None):
    return lax.all_to_all(
        parts, axis, split_axis=0, concat_axis=0, tiled=True, axis_index_groups=groups
    )


def send_on(value, hops):
    peers = lax.axis_size("col")
    return lax.ppermute(value, "col", [(c, (c + hops) % peers) for c in range(peers)])


def on_device(tokens, w1_blocks, w1_coords, w1_count, w2_blocks, w2_coords, w2_count, cotangent):
    peers = lax.axis_size("col")
    far = [[c + NEAR * k for k in range(peers // NEAR)] for c in range(NEAR)]

    own = lax.all_gather(jnp.stack([tokens, cotangent]), "col", axis_index_groups=far)
    own, first, second = lax.optimization_barrier((own, w1_blocks, w2_blocks))
    half = len(far[0]) // 2
    rows = [own] + [
        send_on(part, -step)
        for part, step in zip((own, own, own[:half], own[half:]), STEPS[1:])
    ]
    first, second, table, feature = stage(
        first[0, 0], second[0, 0], w1_coords[0, 0].T, w2_coords[0, 0].T, w1_count, w2_count
    )
    parts = swap(slot_products(rows, first, second, table, feature), "row")
    slots_in = swap(hidden_step(parts), "row")
    sums = feature_sums(slots_in, first, second, feature)
    sums = [sums[0]] + [send_on(part, step) for part, step in zip(sums[1:], STEPS[1:])]
    grads = block_grads(rows, slots_in, feature)
    others = lax.ppermute(grads, "tok", [(0, 1), (1, 0)])
    sums = swap(near_sums(sums), "col", far)
    return final_sums(sums, grads, others)


def solution(mesh):
    placed = (
        P(("tok", "col"), "row"),
        P("row", "col", None, None, None),
        P("row", "col", None, None),
        P("row", "col"),
        P("row", "col", None, None, None),
        P("row", "col", None, None),
        P("row", "col"),
        P(("tok", "col"), "row"),
    )
    return jax.shard_map(
        on_device,
        mesh=mesh,
        in_specs=placed,
        out_specs=(
            P(("tok", "col"), "row"),
            P(("tok", "col"), "row"),
            P("row", "col", None, None, None),
            P("row", "col", None, None, None),
        ),
        check_vma=False,
    )
```

```python
import functools

import jax
import jax.numpy as jnp
from jax import lax
from jax.experimental import pallas as pl
from jax.experimental.pallas import tpu as pltpu
from jax.sharding import PartitionSpec as P

BS = 128
FEATURE = 8
HIDDEN = 32
NEAR = 4
TOTALS = 4
STEPS = (0, 1, -1, 2, -2)
PLACES = (4, 4, 4, 2, 2)
VMEM_BYTES = 12 * 1024 * 1024

VMEM = functools.partial(pl.BlockSpec, memory_space=pltpu.VMEM)
SMEM = functools.partial(pl.BlockSpec, memory_space=pltpu.SMEM)
HBM = functools.partial(pl.BlockSpec, memory_space=pltpu.HBM)


def call(body, in_specs, out_shapes, scratch=(), flops=0, nbytes=0):
    return pl.pallas_call(
        body,
        in_specs=in_specs,
        out_specs=jax.tree.map(lambda _: VMEM(), out_shapes),
        out_shape=out_shapes,
        scratch_shapes=list(scratch),
        compiler_params=pltpu.CompilerParams(vmem_limit_bytes=VMEM_BYTES),
        cost_estimate=pl.CostEstimate(flops=flops, bytes_accessed=nbytes, transcendentals=0),
    )


def product_dims(transpose):
    return (((1,), (1,)), ((), ())) if transpose else (((1,), (0,)), ((), ()))


def block_column(rows_refs, line, index):
    start = pl.multiple_of(index * BS, BS)
    parts = [ref[:, line, :, pl.ds(start, BS)] for ref in rows_refs]
    return jnp.concatenate(parts, axis=0).reshape(-1, BS)


def stage(first, second, first_coords, second_coords, first_count, second_count):
    slots = first.shape[0]

    def body(n1_ref, n2_ref, *refs):
        sources, (w1_ref, w2_ref, table_ref, feature_ref) = refs[:4], refs[4:8]
        c1_ref, c2_ref, sems = refs[8:]
        targets = (c1_ref, c2_ref, w1_ref, w2_ref)
        copies = [
            pltpu.make_async_copy(x, y, sems.at[i]) for i, (x, y) in enumerate(zip(sources, targets))
        ]
        for copy in copies:
            copy.start()
        for copy in copies[:2]:
            copy.wait()
        lane = lax.broadcasted_iota(jnp.int32, table_ref.shape, 1)
        table = jnp.zeros(table_ref.shape, jnp.int32)
        row = lax.broadcasted_iota(jnp.int32, feature_ref.shape, 0)
        place = lax.broadcasted_iota(jnp.int32, feature_ref.shape, 1)
        feature = jnp.zeros(feature_ref.shape, jnp.int32)
        for s in range(slots):
            i = jnp.where(s < n1_ref[0, 0], c1_ref[1, s], HIDDEN)
            j = jnp.where(s < n2_ref[0, 0], c2_ref[0, s], HIDDEN)
            table = jnp.where(lane == s, i, jnp.where(lane == 64 + s, j, table))
            feature = jnp.where(place == s, jnp.where(row == 0, c1_ref[0, s], c2_ref[1, s]), feature)
        table_ref[...] = table.astype(jnp.float32).astype(jnp.bfloat16)
        feature_ref[...] = feature
        for copy in copies[2:]:
            copy.wait()

    return call(
        body,
        [SMEM()] * 2 + [HBM()] * 4,
        (
            jax.ShapeDtypeStruct(first.shape, jnp.bfloat16),
            jax.ShapeDtypeStruct(second.shape, jnp.bfloat16),
            jax.ShapeDtypeStruct((16, BS), jnp.bfloat16),
            jax.ShapeDtypeStruct((8, BS), jnp.int32),
        ),
        scratch=[
            pltpu.SMEM(first_coords.shape, jnp.int32),
            pltpu.SMEM(second_coords.shape, jnp.int32),
            pltpu.SemaphoreType.DMA((4,)),
        ],
        flops=first.size,
        nbytes=8 * first.size,
    )(
        first_count,
        second_count,
        *(
            pltpu.with_memory_space_constraint(value, pltpu.HBM)
            for value in (first_coords, second_coords, first, second)
        ),
    )


def slot_products(rows, first, second, table, feature):
    share = rows[0].shape[2]
    peers = sum(part.shape[0] for part in rows)
    slots = first.shape[0]

    def body(index_ref, table_ref, w1_ref, w2_ref, *refs):
        rows_refs, out_ref = refs[: len(rows)], refs[len(rows)]
        for p in range(peers):
            out_ref[p, 2 * slots] = table_ref[...]
        for base, line, blocks_ref in ((0, 0, w1_ref), (slots, 1, w2_ref)):
            for s in range(slots):
                left = block_column(rows_refs, line, index_ref[line, s])
                product = lax.dot_general(
                    left, blocks_ref[s], product_dims(line > 0), preferred_element_type=jnp.float32
                )
                out_ref[:, base + s] = product.astype(jnp.bfloat16).reshape(peers, share, BS)

    return call(
        body,
        [SMEM()] + [VMEM()] * (len(rows) + 3),
        jax.ShapeDtypeStruct((peers, 2 * slots + 1, share, BS), jnp.bfloat16),
        flops=4 * slots * peers * share * BS * BS,
        nbytes=8 * slots * peers * share * BS,
    )(feature, table, first, second, *rows)


def hidden_step(parts):
    peers, width = parts.shape[0], parts.shape[3]
    slots = parts.shape[1] // 2
    share = parts.shape[2]
    hidden_blocks = HIDDEN

    def body(parts_ref, out_ref, *refs):
        pre, grad = refs[:TOTALS], refs[TOTALS : 2 * TOTALS]
        act_blocks, grad_blocks, table, index, sem = refs[2 * TOTALS :]
        row = lax.broadcasted_iota(jnp.int32, (peers, width), 0)
        lines = jnp.zeros((peers, width), jnp.float32)
        for p in range(peers):
            lines = jnp.where(row == p, parts_ref[p, 2 * slots].astype(jnp.float32), lines)
        table[...] = lines.astype(jnp.int32)
        copy = pltpu.make_async_copy(table, index, sem)
        copy.start()
        for total in pre + grad:
            total[...] = jnp.zeros_like(total)
        act_blocks[hidden_blocks:] = jnp.zeros((1, share, width), jnp.bfloat16)
        grad_blocks[hidden_blocks:] = jnp.zeros((1, share, width), jnp.bfloat16)
        copy.wait()

        def add(p, carry):
            for s in range(slots):
                for t in range(TOTALS):
                    q = p + t * (peers // TOTALS)
                    i, j = index[q, s], index[q, 64 + s]
                    pre[t][i] = pre[t][i] + parts_ref[q, s].astype(jnp.float32)
                    grad[t][j] = grad[t][j] + parts_ref[q, slots + s].astype(jnp.float32)
            return carry

        lax.fori_loop(0, peers // TOTALS, add, 0, unroll=True)

        def point(h, carry):
            value = sum(total[h] for total in pre[1:]) + pre[0][h]
            slope = sum(total[h] for total in grad[1:]) + grad[0][h]
            gate = 1.0 / (1.0 + jnp.exp(-value))
            act_blocks[h] = (value * gate).astype(jnp.bfloat16)
            grad_blocks[h] = (slope * gate * (1.0 + value * (1.0 - gate))).astype(jnp.bfloat16)
            return carry

        lax.fori_loop(0, hidden_blocks, point, 0, unroll=8)

        def pick(p, carry):
            for s in range(slots):
                out_ref[p, s] = act_blocks[index[p, 64 + s]]
                out_ref[p, slots + s] = grad_blocks[index[p, s]]
            return carry

        lax.fori_loop(0, peers, pick, 0, unroll=True)

    return call(
        body,
        [VMEM()],
        jax.ShapeDtypeStruct((peers, 2 * slots, share, width), jnp.bfloat16),
        scratch=[
            *[pltpu.VMEM((hidden_blocks + 1, share, width), jnp.float32)] * (2 * TOTALS),
            pltpu.VMEM((hidden_blocks + 1, share, width), jnp.bfloat16),
            pltpu.VMEM((hidden_blocks + 1, share, width), jnp.bfloat16),
            pltpu.VMEM((peers, width), jnp.int32),
            pltpu.SMEM((peers, width), jnp.int32),
            pltpu.SemaphoreType.DMA,
        ],
        flops=4 * parts.size,
        nbytes=6 * parts.size,
    )(parts)


def feature_sums(slots_in, first, second, feature):
    peers, both, share, width = slots_in.shape
    slots = both // 2

    def body(index_ref, in_ref, w1_ref, w2_ref, *refs):
        out_refs, total = refs[:-1], refs[-1]
        for base, line, blocks_ref in ((0, 1, w2_ref), (slots, 0, w1_ref)):
            total[...] = jnp.zeros_like(total)
            for s in range(slots):
                left = in_ref[:, base + s].reshape(peers * share, width)
                product = lax.dot_general(
                    left, blocks_ref[s], product_dims(base > 0), preferred_element_type=jnp.float32
                )
                target = index_ref[line, s]
                total[target] = total[target] + product
            place = FEATURE if base else 0
            for k in range(FEATURE):
                value = total[k].astype(jnp.bfloat16).reshape(peers, share, width)
                at = 0
                for ref, places in zip(out_refs, PLACES):
                    ref[:, place + k] = value[at : at + places]
                    at += places

    return call(
        body,
        [SMEM()] + [VMEM()] * 3,
        tuple(
            jax.ShapeDtypeStruct((places, 2 * FEATURE, share, width), jnp.bfloat16) for places in PLACES
        ),
        scratch=[pltpu.VMEM((FEATURE, peers * share, width), jnp.float32)],
        flops=2 * slots_in.size * BS,
        nbytes=4 * slots_in.size,
    )(feature, slots_in, first, second)


def block_grads(rows, slots_in, feature):
    peers, both, share, width = slots_in.shape
    slots = both // 2
    dims = (((0,), (0,)), ((), ()))

    def body(index_ref, *refs):
        rows_refs, (in_ref, out_ref) = refs[: len(rows)], refs[len(rows) :]
        for s in range(slots):
            left = block_column(rows_refs, 0, index_ref[0, s])
            hidden = in_ref[:, slots + s].reshape(peers * share, width)
            grad = lax.dot_general(left, hidden, dims, preferred_element_type=jnp.float32)
            out_ref[s] = grad.astype(jnp.bfloat16)
        for s in range(slots):
            right = block_column(rows_refs, 1, index_ref[1, s])
            hidden = in_ref[:, s].reshape(peers * share, width)
            grad = lax.dot_general(hidden, right, dims, preferred_element_type=jnp.float32)
            out_ref[slots + s] = grad.astype(jnp.bfloat16)

    return call(
        body,
        [SMEM()] + [VMEM()] * (len(rows) + 1),
        jax.ShapeDtypeStruct((both, BS, BS), jnp.bfloat16),
        flops=2 * slots_in.size * BS,
        nbytes=4 * slots_in.size,
    )(feature, *rows, slots_in)


def near_sums(parts):
    group, blocks, share, width = parts[0].shape
    half = group // 2

    def body(*refs):
        part_refs, halves, out_ref = refs[:3], refs[3:5], refs[5]
        for k in range(group):
            for b in range(blocks):
                total = halves[k // half][k % half, b].astype(jnp.float32)
                for ref in part_refs:
                    total = total + ref[k, b].astype(jnp.float32)
                out_ref[k, b] = total.astype(jnp.bfloat16)

    return call(
        body,
        [VMEM()] * len(parts),
        jax.ShapeDtypeStruct((group, blocks, share, width), jnp.bfloat16),
        flops=4 * parts[0].size,
        nbytes=8 * parts[0].size,
    )(*parts)


def final_sums(parts, grads, others):
    group, both, share, width = parts.shape
    slots = grads.shape[0] // 2

    def body(parts_ref, grads_ref, others_ref, out_ref, in_ref, w1_ref, w2_ref):
        for s in range(2 * slots):
            total = grads_ref[s].astype(jnp.float32) + others_ref[s].astype(jnp.float32)
            target = w1_ref if s < slots else w2_ref
            target[0, 0, s % slots] = total.astype(jnp.bfloat16)
        for k in range(both):
            total = parts_ref[0, k].astype(jnp.float32)
            for c in range(1, group):
                total = total + parts_ref[c, k].astype(jnp.float32)
            target, place = (out_ref, k) if k < FEATURE else (in_ref, k - FEATURE)
            target[:, place * width : (place + 1) * width] = total.astype(jnp.bfloat16)

    row = jax.ShapeDtypeStruct((share, FEATURE * width), jnp.bfloat16)
    grad = jax.ShapeDtypeStruct((1, 1, slots, BS, BS), jnp.bfloat16)
    return call(
        body, [VMEM()] * 3, (row, row, grad, grad), flops=grads.size, nbytes=6 * grads.size
    )(parts, grads, others)


def swap(parts, axis, groups=None):
    return lax.all_to_all(
        parts, axis, split_axis=0, concat_axis=0, tiled=True, axis_index_groups=groups
    )


def send_on(value, hops):
    peers = lax.axis_size("col")
    return lax.ppermute(value, "col", [(c, (c + hops) % peers) for c in range(peers)])


def on_device(tokens, w1_blocks, w1_coords, w1_count, w2_blocks, w2_coords, w2_count, cotangent):
    peers = lax.axis_size("col")
    far = [[c + NEAR * k for k in range(peers // NEAR)] for c in range(NEAR)]

    own = lax.all_gather(jnp.stack([tokens, cotangent]), "col", axis_index_groups=far)
    own, first, second = lax.optimization_barrier((own, w1_blocks, w2_blocks))
    half = len(far[0]) // 2
    rows = [own] + [
        send_on(part, -step)
        for part, step in zip((own, own, own[:half], own[half:]), STEPS[1:])
    ]
    first, second, table, feature = stage(
        first[0, 0], second[0, 0], w1_coords[0, 0].T, w2_coords[0, 0].T, w1_count, w2_count
    )
    parts = swap(slot_products(rows, first, second, table, feature), "row")
    slots_in = swap(hidden_step(parts), "row")
    sums = feature_sums(slots_in, first, second, feature)
    sums = [sums[0]] + [send_on(part, step) for part, step in zip(sums[1:], STEPS[1:])]
    grads = block_grads(rows, slots_in, feature)
    others = lax.ppermute(grads, "tok", [(0, 1), (1, 0)])
    sums = swap(near_sums(sums), "col", far)
    return final_sums(sums, grads, others)


def solution(mesh):
    placed = (
        P(("tok", "col"), "row"),
        P("row", "col", None, None, None),
        P("row", "col", None, None),
        P("row", "col"),
        P("row", "col", None, None, None),
        P("row", "col", None, None),
        P("row", "col"),
        P(("tok", "col"), "row"),
    )
    return jax.shard_map(
        on_device,
        mesh=mesh,
        in_specs=placed,
        out_specs=(
            P(("tok", "col"), "row"),
            P(("tok", "col"), "row"),
            P("row", "col", None, None, None),
            P("row", "col", None, None, None),
        ),
        check_vma=False,
    )
```

```python
import functools

import jax
import jax.numpy as jnp
from jax import lax
from jax.experimental import pallas as pl
from jax.experimental.pallas import tpu as pltpu
from jax.sharding import PartitionSpec as P

BS = 128
FEATURE = 8
HIDDEN = 32
NEAR = 4
TOTALS = 4
STEPS = (0, 1, -1, 2, -2)
PLACES = (4, 4, 4, 2, 2)
VMEM_BYTES = 12 * 1024 * 1024

VMEM = functools.partial(pl.BlockSpec, memory_space=pltpu.VMEM)
SMEM = functools.partial(pl.BlockSpec, memory_space=pltpu.SMEM)
HBM = functools.partial(pl.BlockSpec, memory_space=pltpu.HBM)


def call(body, in_specs, out_shapes, scratch=(), flops=0, nbytes=0):
    return pl.pallas_call(
        body,
        in_specs=in_specs,
        out_specs=jax.tree.map(lambda _: VMEM(), out_shapes),
        out_shape=out_shapes,
        scratch_shapes=list(scratch),
        compiler_params=pltpu.CompilerParams(vmem_limit_bytes=VMEM_BYTES),
        cost_estimate=pl.CostEstimate(flops=flops, bytes_accessed=nbytes, transcendentals=0),
    )


def product_dims(transpose):
    return (((1,), (1,)), ((), ())) if transpose else (((1,), (0,)), ((), ()))


def block_column(rows_refs, line, index):
    start = pl.multiple_of(index * BS, BS)
    parts = [ref[:, line, :, pl.ds(start, BS)] for ref in rows_refs]
    return jnp.concatenate(parts, axis=0).reshape(-1, BS)


def stage(first, second, first_coords, second_coords, first_count, second_count):
    slots = first.shape[0]

    def body(n1_ref, n2_ref, *refs):
        sources, (w1_ref, w2_ref, table_ref, feature_ref) = refs[:4], refs[4:8]
        c1_ref, c2_ref, sems = refs[8:]
        targets = (c1_ref, c2_ref, w1_ref, w2_ref)
        copies = [
            pltpu.make_async_copy(x, y, sems.at[i]) for i, (x, y) in enumerate(zip(sources, targets))
        ]
        for copy in copies:
            copy.start()
        for copy in copies[:2]:
            copy.wait()
        lane = lax.broadcasted_iota(jnp.int32, table_ref.shape, 1)
        table = jnp.zeros(table_ref.shape, jnp.int32)
        row = lax.broadcasted_iota(jnp.int32, feature_ref.shape, 0)
        place = lax.broadcasted_iota(jnp.int32, feature_ref.shape, 1)
        feature = jnp.zeros(feature_ref.shape, jnp.int32)
        for s in range(slots):
            i = jnp.where(s < n1_ref[0, 0], c1_ref[1, s], HIDDEN)
            j = jnp.where(s < n2_ref[0, 0], c2_ref[0, s], HIDDEN)
            table = jnp.where(lane == s, i, jnp.where(lane == 64 + s, j, table))
            feature = jnp.where(place == s, jnp.where(row == 0, c1_ref[0, s], c2_ref[1, s]), feature)
        table_ref[...] = table.astype(jnp.float32).astype(jnp.bfloat16)
        feature_ref[...] = feature
        for copy in copies[2:]:
            copy.wait()

    return call(
        body,
        [SMEM()] * 2 + [HBM()] * 4,
        (
            jax.ShapeDtypeStruct(first.shape, jnp.bfloat16),
            jax.ShapeDtypeStruct(second.shape, jnp.bfloat16),
            jax.ShapeDtypeStruct((16, BS), jnp.bfloat16),
            jax.ShapeDtypeStruct((8, BS), jnp.int32),
        ),
        scratch=[
            pltpu.SMEM(first_coords.shape, jnp.int32),
            pltpu.SMEM(second_coords.shape, jnp.int32),
            pltpu.SemaphoreType.DMA((4,)),
        ],
        flops=first.size,
        nbytes=8 * first.size,
    )(
        first_count,
        second_count,
        *(
            pltpu.with_memory_space_constraint(value, pltpu.HBM)
            for value in (first_coords, second_coords, first, second)
        ),
    )


def slot_products(rows, first, second, table, feature):
    share = rows[0].shape[2]
    peers = sum(part.shape[0] for part in rows)
    slots = first.shape[0]

    def body(index_ref, table_ref, w1_ref, w2_ref, *refs):
        rows_refs, out_ref = refs[: len(rows)], refs[len(rows)]
        for p in range(peers):
            out_ref[p, 2 * slots] = table_ref[...]
        for base, line, blocks_ref in ((0, 0, w1_ref), (slots, 1, w2_ref)):
            for s in range(slots):
                left = block_column(rows_refs, line, index_ref[line, s])
                product = lax.dot_general(
                    left, blocks_ref[s], product_dims(line > 0), preferred_element_type=jnp.float32
                )
                out_ref[:, base + s] = product.astype(jnp.bfloat16).reshape(peers, share, BS)

    return call(
        body,
        [SMEM()] + [VMEM()] * (len(rows) + 3),
        jax.ShapeDtypeStruct((peers, 2 * slots + 1, share, BS), jnp.bfloat16),
        flops=4 * slots * peers * share * BS * BS,
        nbytes=8 * slots * peers * share * BS,
    )(feature, table, first, second, *rows)


def hidden_step(parts):
    peers, width = parts.shape[0], parts.shape[3]
    slots = parts.shape[1] // 2
    share = parts.shape[2]
    hidden_blocks = HIDDEN

    def body(parts_ref, out_ref, *refs):
        pre, grad = refs[:TOTALS], refs[TOTALS : 2 * TOTALS]
        act_blocks, grad_blocks, table, index, sem = refs[2 * TOTALS :]
        row = lax.broadcasted_iota(jnp.int32, (peers, width), 0)
        lines = jnp.zeros((peers, width), jnp.float32)
        for p in range(peers):
            lines = jnp.where(row == p, parts_ref[p, 2 * slots].astype(jnp.float32), lines)
        table[...] = lines.astype(jnp.int32)
        copy = pltpu.make_async_copy(table, index, sem)
        copy.start()
        for total in pre + grad:
            total[...] = jnp.zeros_like(total)
        act_blocks[hidden_blocks:] = jnp.zeros((1, share, width), jnp.bfloat16)
        grad_blocks[hidden_blocks:] = jnp.zeros((1, share, width), jnp.bfloat16)
        copy.wait()

        def add(p, carry):
            for s in range(slots):
                for t in range(TOTALS):
                    q = p + t * (peers // TOTALS)
                    i, j = index[q, s], index[q, 64 + s]
                    pre[t][i] = pre[t][i] + parts_ref[q, s].astype(jnp.float32)
                    grad[t][j] = grad[t][j] + parts_ref[q, slots + s].astype(jnp.float32)
            return carry

        lax.fori_loop(0, peers // TOTALS, add, 0, unroll=True)

        def point(h, carry):
            value = sum(total[h] for total in pre[1:]) + pre[0][h]
            slope = sum(total[h] for total in grad[1:]) + grad[0][h]
            gate = 1.0 / (1.0 + jnp.exp(-value))
            act_blocks[h] = (value * gate).astype(jnp.bfloat16)
            grad_blocks[h] = (slope * gate * (1.0 + value * (1.0 - gate))).astype(jnp.bfloat16)
            return carry

        lax.fori_loop(0, hidden_blocks, point, 0, unroll=8)

        def pick(p, carry):
            for s in range(slots):
                out_ref[p, s] = act_blocks[index[p, 64 + s]]
                out_ref[p, slots + s] = grad_blocks[index[p, s]]
            return carry

        lax.fori_loop(0, peers, pick, 0, unroll=True)

    return call(
        body,
        [VMEM()],
        jax.ShapeDtypeStruct((peers, 2 * slots, share, width), jnp.bfloat16),
        scratch=[
            *[pltpu.VMEM((hidden_blocks + 1, share, width), jnp.float32)] * (2 * TOTALS),
            pltpu.VMEM((hidden_blocks + 1, share, width), jnp.bfloat16),
            pltpu.VMEM((hidden_blocks + 1, share, width), jnp.bfloat16),
            pltpu.VMEM((peers, width), jnp.int32),
            pltpu.SMEM((peers, width), jnp.int32),
            pltpu.SemaphoreType.DMA,
        ],
        flops=4 * parts.size,
        nbytes=6 * parts.size,
    )(parts)


def feature_sums(slots_in, first, second, feature):
    peers, both, share, width = slots_in.shape
    slots = both // 2

    def body(index_ref, in_ref, w1_ref, w2_ref, *refs):
        out_refs, total = refs[:-1], refs[-1]
        for base, line, blocks_ref in ((0, 1, w2_ref), (slots, 0, w1_ref)):
            total[...] = jnp.zeros_like(total)
            for s in range(slots):
                left = in_ref[:, base + s].reshape(peers * share, width)
                product = lax.dot_general(
                    left, blocks_ref[s], product_dims(base > 0), preferred_element_type=jnp.float32
                )
                target = index_ref[line, s]
                total[target] = total[target] + product
            place = FEATURE if base else 0
            for k in range(FEATURE):
                value = total[k].astype(jnp.bfloat16).reshape(peers, share, width)
                at = 0
                for ref, places in zip(out_refs, PLACES):
                    ref[:, place + k] = value[at : at + places]
                    at += places

    return call(
        body,
        [SMEM()] + [VMEM()] * 3,
        tuple(
            jax.ShapeDtypeStruct((places, 2 * FEATURE, share, width), jnp.bfloat16) for places in PLACES
        ),
        scratch=[pltpu.VMEM((FEATURE, peers * share, width), jnp.float32)],
        flops=2 * slots_in.size * BS,
        nbytes=4 * slots_in.size,
    )(feature, slots_in, first, second)


def block_grads(rows, slots_in, feature):
    peers, both, share, width = slots_in.shape
    slots = both // 2
    dims = (((0,), (0,)), ((), ()))

    def body(index_ref, *refs):
        rows_refs, (in_ref, out_ref) = refs[: len(rows)], refs[len(rows) :]
        for s in range(slots):
            left = block_column(rows_refs, 0, index_ref[0, s])
            hidden = in_ref[:, slots + s].reshape(peers * share, width)
            grad = lax.dot_general(left, hidden, dims, preferred_element_type=jnp.float32)
            out_ref[s] = grad.astype(jnp.bfloat16)
        for s in range(slots):
            right = block_column(rows_refs, 1, index_ref[1, s])
            hidden = in_ref[:, s].reshape(peers * share, width)
            grad = lax.dot_general(hidden, right, dims, preferred_element_type=jnp.float32)
            out_ref[slots + s] = grad.astype(jnp.bfloat16)

    return call(
        body,
        [SMEM()] + [VMEM()] * (len(rows) + 1),
        jax.ShapeDtypeStruct((both, BS, BS), jnp.bfloat16),
        flops=2 * slots_in.size * BS,
        nbytes=4 * slots_in.size,
    )(feature, *rows, slots_in)


def near_sums(parts):
    group, blocks, share, width = parts[0].shape
    half = group // 2

    def body(*refs):
        part_refs, halves, out_ref = refs[:3], refs[3:5], refs[5]
        for k in range(group):
            for b in range(blocks):
                total = halves[k // half][k % half, b].astype(jnp.float32)
                for ref in part_refs:
                    total = total + ref[k, b].astype(jnp.float32)
                out_ref[k, b] = total.astype(jnp.bfloat16)

    return call(
        body,
        [VMEM()] * len(parts),
        jax.ShapeDtypeStruct((group, blocks, share, width), jnp.bfloat16),
        flops=4 * parts[0].size,
        nbytes=8 * parts[0].size,
    )(*parts)


def final_sums(parts, grads, others):
    group, both, share, width = parts.shape
    slots = grads.shape[0] // 2

    def body(parts_ref, grads_ref, others_ref, out_ref, in_ref, w1_ref, w2_ref):
        for s in range(2 * slots):
            total = grads_ref[s].astype(jnp.float32) + others_ref[s].astype(jnp.float32)
            target = w1_ref if s < slots else w2_ref
            target[0, 0, s % slots] = total.astype(jnp.bfloat16)
        for k in range(both):
            total = parts_ref[0, k].astype(jnp.float32)
            for c in range(1, group):
                total = total + parts_ref[c, k].astype(jnp.float32)
            target, place = (out_ref, k) if k < FEATURE else (in_ref, k - FEATURE)
            target[:, place * width : (place + 1) * width] = total.astype(jnp.bfloat16)

    row = jax.ShapeDtypeStruct((share, FEATURE * width), jnp.bfloat16)
    grad = jax.ShapeDtypeStruct((1, 1, slots, BS, BS), jnp.bfloat16)
    return call(
        body, [VMEM()] * 3, (row, row, grad, grad), flops=grads.size, nbytes=6 * grads.size
    )(parts, grads, others)


def swap(parts, axis, groups=None):
    return lax.all_to_all(
        parts, axis, split_axis=0, concat_axis=0, tiled=True, axis_index_groups=groups
    )


def send_on(value, hops):
    peers = lax.axis_size("col")
    return lax.ppermute(value, "col", [(c, (c + hops) % peers) for c in range(peers)])


def on_device(tokens, w1_blocks, w1_coords, w1_count, w2_blocks, w2_coords, w2_count, cotangent):
    peers = lax.axis_size("col")
    far = [[c + NEAR * k for k in range(peers // NEAR)] for c in range(NEAR)]

    own = lax.all_gather(jnp.stack([tokens, cotangent]), "col", axis_index_groups=far)
    own, first, second = lax.optimization_barrier((own, w1_blocks, w2_blocks))
    half = len(far[0]) // 2
    rows = [own] + [
        send_on(part, -step)
        for part, step in zip((own, own, own[:half], own[half:]), STEPS[1:])
    ]
    first, second, table, feature = stage(
        first[0, 0], second[0, 0], w1_coords[0, 0].T, w2_coords[0, 0].T, w1_count, w2_count
    )
    parts = swap(slot_products(rows, first, second, table, feature), "row")
    slots_in = swap(hidden_step(parts), "row")
    sums = feature_sums(slots_in, first, second, feature)
    sums = [sums[0]] + [send_on(part, step) for part, step in zip(sums[1:], STEPS[1:])]
    sums = near_sums(sums)
    sums, slots_in = lax.optimization_barrier((sums, slots_in))
    grads = block_grads(rows, slots_in, feature)
    others = lax.ppermute(grads, "tok", [(0, 1), (1, 0)])
    sums = swap(sums, "col", far)
    return final_sums(sums, grads, others)


def solution(mesh):
    placed = (
        P(("tok", "col"), "row"),
        P("row", "col", None, None, None),
        P("row", "col", None, None),
        P("row", "col"),
        P("row", "col", None, None, None),
        P("row", "col", None, None),
        P("row", "col"),
        P(("tok", "col"), "row"),
    )
    return jax.shard_map(
        on_device,
        mesh=mesh,
        in_specs=placed,
        out_specs=(
            P(("tok", "col"), "row"),
            P(("tok", "col"), "row"),
            P("row", "col", None, None, None),
            P("row", "col", None, None, None),
        ),
        check_vma=False,
    )
```
